128 devices in a mesh: fsdp: 8 (over y, z_hi), tsp: 16 (over x, z_lo, core).
Axes of the slice: x: 4, y: 4, z: 4 (z_hi: 2, z_lo: 2; z = z_hi * 2 + z_lo), core: 2. Of those that a mesh axis runs over, the one named last changes fastest.
Arguments:
- tokens: bfloat16 [2048, 4096], P(('fsdp', 'tsp')), may hold values from -24 to 24
- out_grad: bfloat16 [2048, 4096], P(('fsdp', 'tsp')), may hold values from -24 to 24
- gate_weight: bfloat16 [4096, 14336], P('fsdp', 'tsp'), may hold values from -0.09375 to 0.09375
- up_weight: bfloat16 [4096, 14336], P('fsdp', 'tsp'), may hold values from -0.09375 to 0.09375
- down_weight: bfloat16 [14336, 4096], P('tsp', 'fsdp'), may hold values from -0.046875 to 0.046875
Outputs:
- input_grad: bfloat16 [2048, 4096], P(('fsdp', 'tsp'))
- gate_grad: float32 [4096, 14336], P('fsdp', 'tsp')
- up_grad: float32 [4096, 14336], P('fsdp', 'tsp')
- down_grad: float32 [14336, 4096], P('tsp', 'fsdp')
The draws below stay inside these ranges and needn't reach their ends.
All inputs are finite; a program needn't handle non-finite values.
Results may differ from the reference program's by a relative error of at most 0.022.
Values may be sent and summed in bfloat16 or wider, within the bound.
No kernel may reach another device: no remote copies, remote signals or barrier semaphores. Data moves between devices by JAX's collectives and lax.ppermute only.
A program may use at most 192 MiB of HBM per device.

```python
import jax
import jax.numpy as jnp
from jax import lax

D = 4096
FF = 14336
TOK_DEV = 256
TOKENS = 2048
N_FSDP = 8
N_TSP = 16


def raised(result, stream_key, source, target, blocks, factor):
    def block_of(axis_at):
        return (jnp.arange(result.shape[axis_at]) // (result.shape[axis_at] // blocks)).reshape((-1,) + (1,) * (result.ndim - 1 - axis_at))

    first = jax.random.permutation(stream_key, blocks)[block_of(target)]
    second = (block_of(target) + blocks // 2) % blocks
    return jnp.where((block_of(source) == first) | (block_of(source) == second), factor * result, result)


def level_of(rng, extent, cuts, least, high):
    gain = 1.0
    for axis_at, blocks in cuts:
        draws = jax.random.uniform(jax.random.fold_in(jax.random.fold_in(rng, 6), axis_at), (blocks,), jnp.float32, least / len(cuts), high / len(cuts))
        gain = gain * jnp.repeat(jnp.exp(draws), extent[axis_at] // blocks).reshape((-1,) + (1,) * (len(extent) - 1 - axis_at))
    return gain


def noise(key, dims, scale, bound, split=(), dtype=jnp.bfloat16):
    gain = level_of(key, dims, split, -0.22, 0.18) if split else 1.0
    array = jax.random.normal(key, dims, jnp.float32) * scale * gain
    return jnp.minimum(jnp.maximum(array, -bound), bound).astype(dtype)


def noise_with(stream_key, shape, spread, reach, pieces, heavy, kind=jnp.bfloat16):
    array = spread * jax.random.normal(stream_key, shape, jnp.float32)
    if pieces:
        array = array * level_of(stream_key, shape, pieces, -0.22, 0.18)
    return jnp.clip(raised(array, jax.random.fold_in(stream_key, 3), *heavy), -reach, reach).astype(kind)


def setup_inputs(seed: int = 0) -> dict:
    key_list = jax.random.split(jax.random.key(seed), 6)
    return {
        "tokens": noise_with(key_list[0], (TOKENS, D), 1.0, 24.0, ((0, 128),), (0, 1, 128, 5.5)),
        "out_grad": noise_with(key_list[1], (TOKENS, D), 1.0, 24.0, ((0, 128),), (0, 1, 128, 5.5)),
        "gate_weight": noise(key_list[2], (D, FF), D ** -0.5, 0.09375, ((0, 8), (1, 16))),
        "up_weight": noise(key_list[3], (D, FF), D ** -0.5, 0.09375, ((0, 8), (1, 16))),
        "down_weight": noise(key_list[4], (FF, D), FF ** -0.5, 0.046875, ((0, 16), (1, 8))),
    }


def reference(tokens, out_grad, gate_weight, up_weight, down_weight):
    gate_pre = jnp.dot(tokens, gate_weight, preferred_element_type=jnp.float32)
    up_pre = jnp.dot(tokens, up_weight, preferred_element_type=jnp.float32)
    sigmoid_gate = jax.nn.sigmoid(gate_pre)
    activated = gate_pre * sigmoid_gate
    hidden = (activated * up_pre).astype(jnp.bfloat16)
    hidden_grad = jnp.dot(out_grad, down_weight.T, preferred_element_type=jnp.float32)
    gate_pgrad = (hidden_grad * up_pre * sigmoid_gate * (1.0 + gate_pre * (1.0 - sigmoid_gate))).astype(jnp.bfloat16)
    up_pgrad = (hidden_grad * activated).astype(jnp.bfloat16)
    width_block = FF // N_TSP
    input_sum = jnp.zeros((TOKENS, D), jnp.float32)
    for block in range(N_TSP):
        lower = block * width_block
        upper = lower + width_block
        partial_sum = jnp.dot(gate_pgrad[:, lower:upper], gate_weight[:, lower:upper].T, preferred_element_type=jnp.float32)
        partial_sum = partial_sum + jnp.dot(up_pgrad[:, lower:upper], up_weight[:, lower:upper].T, preferred_element_type=jnp.float32)
        rounded = lax.optimization_barrier(partial_sum.astype(jnp.bfloat16))
        input_sum = input_sum + rounded.astype(jnp.float32)
    gate_grad = jnp.zeros((D, FF), jnp.float32)
    up_grad = jnp.zeros((D, FF), jnp.float32)
    down_grad = jnp.zeros((FF, D), jnp.float32)
    for group in range(N_FSDP):
        lower = group * TOK_DEV
        upper = lower + TOK_DEV
        tok_group = tokens[lower:upper]
        term_gate = jnp.dot(tok_group.T, gate_pgrad[lower:upper], preferred_element_type=jnp.float32)
        term_up = jnp.dot(tok_group.T, up_pgrad[lower:upper], preferred_element_type=jnp.float32)
        term_down = jnp.dot(hidden[lower:upper].T, out_grad[lower:upper], preferred_element_type=jnp.float32)
        term_gate = lax.optimization_barrier(term_gate.astype(jnp.bfloat16))
        term_up = lax.optimization_barrier(term_up.astype(jnp.bfloat16))
        term_down = lax.optimization_barrier(term_down.astype(jnp.bfloat16))
        gate_grad = gate_grad + term_gate.astype(jnp.float32)
        up_grad = up_grad + term_up.astype(jnp.float32)
        down_grad = down_grad + term_down.astype(jnp.float32)
    return input_sum.astype(jnp.bfloat16), gate_grad, up_grad, down_grad
```

```python
import jax
import jax.numpy as jnp
from jax import lax
from jax.sharding import Mesh, PartitionSpec as P

BF = jnp.bfloat16
F32 = jnp.float32


def shift(value, axis, size, by):
    return lax.ppermute(value, axis, [(i, (i + by) % size) for i in range(size)])


def swap(value, axis):
    return shift(value, axis, 2, 1)


def dot(left, right, dims):
    return lax.dot_general(left, right, (dims, ((), ())), preferred_element_type=F32)


def gather_rows(rows, y, z_hi):
    cols = rows.reshape(16, 4, 2, 512)
    cols = jnp.where(z_hi == 0, cols, cols[:, :, ::-1])
    twice = jnp.concatenate([cols, cols], axis=1)
    rolled = lax.dynamic_slice_in_dim(twice, y, 4, axis=1).reshape(16, 4, 1024)
    parts = [rolled[:, 0]] + [shift(rolled[:, (4 - j) % 4], "y", 4, -j) for j in (1, 2, 3)]
    block = jnp.concatenate(parts, axis=0)
    block = jnp.concatenate([block, swap(block, "z_lo")], axis=0)
    block = jnp.concatenate([block] + [shift(block, "x", 4, -j) for j in (1, 2, 3)], axis=0)
    block = jnp.concatenate([block, swap(block, "core")], axis=0)
    return block.reshape(16, 4, 16, 1024).transpose(1, 0, 2, 3).reshape(4, 256, 1024)


def sum_over_y(blocks):
    own, plus, two, minus = blocks
    low = shift(two[:128], "y", 4, 1)
    high = shift(two[128:], "y", 4, -1)
    plus = jnp.concatenate([(plus[:128].astype(F32) + low.astype(F32)).astype(BF), plus[128:]])
    minus = jnp.concatenate([minus[:128], (minus[128:].astype(F32) + high.astype(F32)).astype(BF)])
    from_low = shift(plus, "y", 4, 1)
    from_high = shift(minus, "y", 4, -1)
    return own.astype(F32) + from_low.astype(F32) + from_high.astype(F32)


def gather_over_y(own):
    minus = shift(own, "y", 4, 1)
    plus = shift(own, "y", 4, -1)
    low = shift(minus[:128], "y", 4, 1)
    high = shift(plus[128:], "y", 4, -1)
    return jnp.concatenate([own, plus, low, high, minus])


def scatter_rows(partial, y, z_hi):
    part = partial.reshape(4, 2, 128, 1024)
    part = part[:, 0] + swap(part[:, 1], "core").astype(F32)
    part = part.astype(BF).reshape(4, 4, 32, 1024)
    total = part[:, 0].astype(F32)
    for j in (1, 2, 3):
        total += shift(part[:, j], "x", 4, j).astype(F32)
    part = total.astype(BF).reshape(4, 2, 16, 1024)
    part = part[:, 0].astype(F32) + swap(part[:, 1], "z_lo").astype(F32)
    part = part.astype(BF)
    cols = [part[0]] + [shift(part[j], "y", 4, j) for j in (1, 2, 3)]
    rolled = jnp.stack([cols[(4 - j) % 4] for j in range(4)], axis=1)
    twice = jnp.concatenate([rolled, rolled], axis=1)
    cols = lax.dynamic_slice_in_dim(twice, (4 - y) % 4, 4, axis=1).reshape(16, 4, 2, 512)
    cols = jnp.where(z_hi == 0, cols, cols[:, :, ::-1])
    return cols.reshape(16, 4096)


def local(tokens, out_grad, gate_weight, up_weight, down_weight):
    y, z_hi = lax.axis_index("y"), lax.axis_index("z_hi")
    gate_other = swap(gate_weight, "z_hi")
    up_other = swap(up_weight, "z_hi")
    down_other = swap(down_weight, "z_hi")
    rows = gather_rows(tokens, y, z_hi)
    cotan = gather_rows(out_grad, y, z_hi)
    rows_flat = rows.reshape(1024, 1024)
    cotan_flat = cotan.reshape(1024, 1024)
    gate_full = jnp.concatenate([gate_weight, gate_other], axis=0)
    up_full = jnp.concatenate([up_weight, up_other], axis=0)
    down_full = jnp.concatenate([down_weight, down_other], axis=1)

    gate_part = dot(rows_flat, gate_full, ((1,), (0,))).astype(BF).reshape(4, 256, 896)
    gate_pre = sum_over_y(gate_part)
    up_part = dot(rows_flat, up_full, ((1,), (0,))).astype(BF).reshape(4, 256, 896)
    up_pre = sum_over_y(up_part)
    grad_part = dot(cotan_flat, down_full, ((1,), (1,))).astype(BF).reshape(4, 256, 896)
    hidden_grad = sum_over_y(grad_part)

    sigmoid_gate = jax.nn.sigmoid(gate_pre)
    activated = gate_pre * sigmoid_gate
    hidden = (activated * up_pre).astype(BF)
    gate_pgrad = (hidden_grad * up_pre * sigmoid_gate * (1.0 + gate_pre * (1.0 - sigmoid_gate))).astype(BF)
    up_pgrad = (hidden_grad * activated).astype(BF)

    gate_all = gather_over_y(gate_pgrad)
    up_all = gather_over_y(up_pgrad)
    hidden_all = gather_over_y(hidden)

    def weight_grad(left, right):
        own = dot(left[:, :512], right, ((0,), (0,)))
        other = dot(left[:, 512:], right, ((0,), (0,))).astype(BF)
        return own + swap(other, "z_hi").astype(F32)

    gate_grad = weight_grad(rows_flat, gate_all)
    up_grad = weight_grad(rows_flat, up_all)
    down_own = dot(hidden_all, cotan_flat[:, :512], ((0,), (0,)))
    down_other = dot(hidden_all, cotan_flat[:, 512:], ((0,), (0,))).astype(BF)
    down_grad = down_own + swap(down_other, "z_hi").astype(F32)

    partial = dot(gate_all, gate_full, ((1,), (1,))) + dot(up_all, up_full, ((1,), (1,)))
    input_grad = scatter_rows(partial.astype(BF), y, z_hi)
    return input_grad, gate_grad, up_grad, down_grad


def solution(mesh):
    split = Mesh(mesh.devices.reshape(4, 2, 4, 2, 2), ("y", "z_hi", "x", "z_lo", "core"))
    fsdp, tsp = ("y", "z_hi"), ("x", "z_lo", "core")
    rows = P(fsdp + tsp, None)
    in_specs = (rows, rows, P(fsdp, tsp), P(fsdp, tsp), P(tsp, fsdp))
    out_specs = (rows, P(fsdp, tsp), P(fsdp, tsp), P(tsp, fsdp))
    return jax.shard_map(local, mesh=split, in_specs=in_specs, out_specs=out_specs, check_vma=False)
```

```python
import jax
import jax.numpy as jnp
from jax import lax
from jax.experimental import pallas as pl
from jax.experimental.pallas import tpu as pltpu
from jax.sharding import Mesh, PartitionSpec as P

BF = jnp.bfloat16
F32 = jnp.float32
SPLIT = 512
LIMIT = 20 * 1024 * 1024


def shift(value, axis, size, by):
    return lax.ppermute(value, axis, [(i, (i + by) % size) for i in range(size)])


def swap(value, axis):
    return shift(value, axis, 2, 1)


def after(value, *earlier):
    return lax.optimization_barrier((value,) + earlier)[0]


def dot(left, right, dims):
    return lax.dot_general(left, right, (dims, ((), ())), preferred_element_type=F32)


def kernel_call(body, shapes, *operands):
    spec = pl.BlockSpec(memory_space=pltpu.VMEM)
    return pl.pallas_call(
        body,
        out_shape=[jax.ShapeDtypeStruct(shape, kind) for shape, kind in shapes],
        in_specs=[spec] * len(operands),
        out_specs=[spec] * len(shapes),
        compiler_params=pltpu.CompilerParams(vmem_limit_bytes=LIMIT),
    )(*operands)


def feature_groups(pieces):
    rows = pieces[0].shape[0]

    def body(*refs):
        y, z_hi = lax.axis_index("y"), lax.axis_index("z_hi")
        for k in range(4):
            for half in range(2):
                at = pl.multiple_of(lax.rem(y + k, 4) * 1024 + lax.rem(z_hi + half, 2) * 512, 512)
                for i in range(len(pieces)):
                    refs[len(pieces) + k][i * rows : (i + 1) * rows, half * 512 : (half + 1) * 512] = refs[i][
                        :, pl.ds(at, 512)
                    ]

    return kernel_call(body, [((rows * len(pieces), 1024), BF)] * 4, *pieces)


def whole_rows(groups):
    def body(*refs):
        y, z_hi = lax.axis_index("y"), lax.axis_index("z_hi")
        for k in range(4):
            for half in range(2):
                at = pl.multiple_of(lax.rem(y + 4 - k, 4) * 1024 + lax.rem(z_hi + half, 2) * 512, 512)
                refs[4][:, pl.ds(at, 512)] = refs[k][:, half * 512 : (half + 1) * 512]

    return kernel_call(body, [((16, 4096), BF)], *groups)[0]


def split_tokens(parts):
    def body(*refs):
        for y in range(4):
            for z in range(2):
                for which in range(2):
                    to = y * 32 + z * 16
                    at = z * 32 + which * 16
                    refs[4 + which][to : to + 16] = refs[y][at : at + 16]

    return kernel_call(body, [((128, 1024), BF)] * 2, *parts)


def assemble_tokens(pieces):
    def body(*refs):
        for y in range(4):
            for i in range(8):
                refs[8][y * 256 + i * 32 : y * 256 + (i + 1) * 32] = refs[i][y * 32 : (y + 1) * 32]

    return kernel_call(body, [((1024, 1024), BF)], *pieces)[0]


def forward(groups):
    plan, flat, total = [], [], 0
    for rows, turned, weights in groups:
        at = len(flat)
        flat.append(rows)
        for pair in weights:
            width = pair[0].shape[0 if turned else 1]
            plan.append((at, len(flat), turned, total, total + width))
            flat.extend(pair)
            total += width

    def body(*refs):
        own, up, down, low, high = refs[len(flat) :]
        for rows_at, pair_at, turned, start, stop in plan:
            cols = slice(start, stop)
            dims = (((1,), (1,)), ((), ())) if turned else (((1,), (0,)), ((), ()))
            for block in (2, 1, 3, 0):
                at = refs[rows_at][block * 256 : (block + 1) * 256]
                out = lax.dot_general(at[:, :512], refs[pair_at][...], dims, preferred_element_type=F32)
                out += lax.dot_general(at[:, 512:], refs[pair_at + 1][...], dims, preferred_element_type=F32)
                out = out.astype(BF)
                if block == 0:
                    own[:, cols] = out
                elif block == 1:
                    low[:, cols] = out[:128]
                    up[128:, cols] = out[128:]
                elif block == 2:
                    up[:128, cols] = out[:128]
                    down[:128, cols] = out[128:]
                else:
                    down[128:, cols] = out[:128]
                    high[:, cols] = out[128:]

    shapes = [((n, total), BF) for n in (256, 256, 256, 128, 128)]
    return kernel_call(body, shapes, *flat)


def add(left, right):
    return (left.astype(F32) + right.astype(F32)).astype(BF)


def ring_first(terms):
    return shift(terms[1], "y", 4, 1), shift(terms[2], "y", 4, -1)


def ring_second(terms, first):
    return shift(add(terms[3], first[0][:128]), "y", 4, 1), shift(add(terms[4], first[1][:128]), "y", 4, -1)


def ring_sum(terms, first, second):
    own = terms[0].astype(F32)
    low = own[:128] + first[1][128:].astype(F32) + second[0].astype(F32)
    high = own[128:] + first[0][128:].astype(F32) + second[1].astype(F32)
    return jnp.concatenate([low, high])


def spread_first(own):
    return shift(own, "y", 4, 1), shift(own, "y", 4, -1)


def spread_second(first):
    return shift(first[0][:128], "y", 4, 1), shift(first[1][128:], "y", 4, -1)


def spread_all(own, first, second):
    return jnp.concatenate([own, first[1], second[0], second[1], first[0]])


def pointwise(gate_pre, up_pre, hidden_grad):
    sigmoid_gate = jax.nn.sigmoid(gate_pre)
    activated = gate_pre * sigmoid_gate
    hidden = activated * up_pre
    gate_pgrad = hidden_grad * up_pre * sigmoid_gate * (1.0 + gate_pre * (1.0 - sigmoid_gate))
    up_pgrad = hidden_grad * activated
    return gate_pgrad.astype(BF), up_pgrad.astype(BF), hidden.astype(BF)


def split_core(parts):
    def body(*refs):
        outs = refs[len(parts) :]
        for half in range(2):
            cols = slice(half * 512, (half + 1) * 512)
            for y in range(4):
                for core in range(2):
                    at = slice(y * 256 + core * 128, y * 256 + core * 128 + 128)
                    total = refs[half][at]
                    for i in range(2 + half, len(parts), 2):
                        total += refs[i][at]
                    if core == 0:
                        outs[0][y * 128 : (y + 1) * 128, cols] = total.astype(BF)
                    else:
                        outs[1 + y][:, cols] = total.astype(BF)

    return kernel_call(body, [((512, 1024), BF)] + [((128, 1024), BF)] * 4, *parts)


def sum_core(keep, got):
    def body(*refs):
        for y in range(4):
            for x in range(4):
                total = refs[0][y * 128 + x * 32 : y * 128 + (x + 1) * 32].astype(F32)
                total += refs[1 + y][x * 32 : (x + 1) * 32].astype(F32)
                refs[5 + x][y * 32 : (y + 1) * 32] = total.astype(BF)

    return kernel_call(body, [((128, 1024), BF)] * 4, keep, *got)


def sum_and_split(parts, rows, ways):
    def body(*refs):
        for y in range(4):
            for way in range(ways):
                at = slice((y * ways + way) * rows, (y * ways + way + 1) * rows)
                total = refs[0][at].astype(F32)
                for i in range(1, len(parts)):
                    total += refs[i][at].astype(F32)
                refs[len(parts) + way][y * rows : (y + 1) * rows] = total.astype(BF)

    return kernel_call(body, [((4 * rows, 1024), BF)] * ways, *parts)


def add_to_rows(keep, got):
    def body(*refs):
        for y in range(4):
            at = slice(y * 16, (y + 1) * 16)
            refs[2 + y][...] = (refs[0][at].astype(F32) + refs[1][at].astype(F32)).astype(BF)

    return kernel_call(body, [((16, 1024), BF)] * 4, keep, got)


def final_add(own, other, axis):
    n = len(own)
    shape = list(own[0].shape)
    shape[axis] = sum(o.shape[axis] for o in own)

    def body(*refs):
        start = 0
        for i in range(n):
            stop = start + own[i].shape[axis]
            at = (slice(None), slice(start, stop)) if axis else (slice(start, stop), slice(None))
            refs[2 * n][at] = refs[i][...] + refs[n + i][...].astype(F32)
            start = stop

    return kernel_call(body, [(tuple(shape), F32)], *own, *other)[0]


def together(first, *earlier):
    first = tuple(first)
    return lax.optimization_barrier(first + earlier)[: len(first)]


def local(tokens, out_grad, gate_weight, up_weight, down_weight):
    gate = [gate_weight[:, :SPLIT], gate_weight[:, SPLIT:]]
    up = [up_weight[:, :SPLIT], up_weight[:, SPLIT:]]
    down = [down_weight[:SPLIT], down_weight[SPLIT:]]

    both = jnp.concatenate([tokens, out_grad], axis=0)
    both_z = swap(both, "z_lo")
    gate_a = swap(after(gate[0], both_z), "z_hi")
    up_a = swap(after(up[0], both_z), "z_hi")
    groups = feature_groups([both, both_z])
    parts = [groups[0]] + [shift(groups[4 - j], "y", 4, -j) for j in (1, 2, 3)]
    tok, cot = split_tokens(parts)
    tok = after(tok, gate_a)
    tok_x = [tok] + [shift(tok, "x", 4, -j) for j in (1, 2, 3)]
    tok_x = list(together(tok_x, up_a))
    cot = after(cot, *tok_x)
    down_a = swap(after(down[0], gate_a), "z_hi")
    cot_x = [cot] + [shift(cot, "x", 4, -j) for j in (1, 2, 3)]
    tok_c = [swap(t, "core") for t in tok_x]
    rows = assemble_tokens(tok_x + tok_c)
    pair_a = forward([(rows, False, [(gate[0], gate_a), (up[0], up_a)])])
    gate_b = swap(after(gate[1], up_a), "z_hi")
    first_p = ring_first(pair_a)
    cot_x = list(together(cot_x, pair_a[0], down_a))
    up_b = swap(after(up[1], down_a), "z_hi")
    cot_c = [swap(t, "core") for t in cot_x]
    first_p = together(first_p, *cot_c)
    cotan = assemble_tokens(cot_x + list(together(cot_c, *first_p)))
    grad_a = forward([(cotan, True, [(down[0], down_a)])])
    first_g = ring_first(grad_a)
    first_p = together(first_p, gate_b)
    second_p = ring_second(pair_a, first_p)
    down_b = swap(after(down[1], gate_b), "z_hi")
    first_g = together(first_g, up_b)
    second_g = ring_second(grad_a, first_g)
    pre_a = ring_sum(pair_a, first_p, second_p)
    hidden_a = ring_sum(grad_a, first_g, second_g)
    gate_pg, up_pg, hid_a = pointwise(pre_a[:, :SPLIT], pre_a[:, SPLIT:], hidden_a)
    own_a = jnp.concatenate([gate_pg, up_pg], axis=1)
    own_a = after(own_a, down_b)
    spread_a = spread_first(own_a)
    all_b = forward([(rows, False, [(gate[1], gate_b), (up[1], up_b)]), (cotan, True, [(down[1], down_b)])])
    first_b = ring_first(all_b)
    spread_a = together(spread_a, all_b[0])
    far_a = spread_second(spread_a)
    first_b = together(first_b, *far_a)
    second_b = ring_second(all_b, first_b)
    spread_h = spread_first(after(hid_a, *spread_a))
    second_b = together(second_b, *spread_h)
    far_h = spread_second(spread_h)
    gu_a = spread_all(own_a, spread_a, far_a)

    def input_terms(pgrads, gate_x, up_x):
        width = gate_x[0].shape[1]
        return [
            dot(pgrads[:, :width], g, ((1,), (1,))) + dot(pgrads[:, width:], u, ((1,), (1,)))
            for g, u in zip(gate_x, up_x)
        ]

    pair_far = dot(rows[:, 512:], gu_a, ((0,), (0,))).astype(BF)
    pair_got_a = swap(pair_far, "z_hi")
    pair_own_a = dot(rows[:, :512], gu_a, ((0,), (0,)))
    input_a = input_terms(gu_a, (gate[0], gate_a), (up[0], up_a))
    total_b = ring_sum(all_b, first_b, second_b)
    width = 896 - SPLIT
    gate_pg, up_pg, hid_b = pointwise(total_b[:, :width], total_b[:, width : 2 * width], total_b[:, 2 * width :])
    own_b = jnp.concatenate([gate_pg, up_pg], axis=1)
    own_b = after(own_b, *far_h)
    hid_all_a = spread_all(hid_a, spread_h, far_h)
    down_far = dot(hid_all_a, cotan[:, 512:], ((0,), (0,))).astype(BF)
    down_got_a = swap(down_far, "z_hi")
    spread_b = spread_first(own_b)
    spread_h = spread_first(after(hid_b, own_b))
    spread_b = together(spread_b, pair_got_a)
    far_b = spread_second(spread_b)
    gu_b = spread_all(own_b, spread_b, far_b)
    gate_far = dot(rows[:, 512:], gu_b[:, :width], ((0,), (0,))).astype(BF)
    up_far = dot(rows[:, 512:], gu_b[:, width:], ((0,), (0,))).astype(BF)
    gate_got_b = swap(gate_far, "z_hi")
    up_got_b = swap(up_far, "z_hi")
    gu_b = after(gu_b, gate_far, up_far)
    input_b = input_terms(gu_b, (gate[1], gate_b), (up[1], up_b))
    gate_got_b = after(gate_got_b, down_got_a)
    keep, *send = split_core(input_a + input_b)
    by_x = sum_core(keep, [swap(part, "core") for part in send])
    by_x = together(by_x, gate_got_b, *spread_h)
    far_h = spread_second(spread_h)
    got = [shift(by_x[j], "x", 4, j) for j in (1, 2, 3)]
    got = together(got, *far_h)
    keep, send = sum_and_split([by_x[0]] + list(got), 16, 2)
    hid_all_b = spread_all(hid_b, spread_h, far_h)
    down_far = dot(hid_all_b, cotan[:, 512:], ((0,), (0,))).astype(BF)
    down_got_b = swap(down_far, "z_hi")
    send = after(send, up_got_b, down_got_b)
    got_z = swap(send, "z_lo")
    by_y = add_to_rows(keep, got_z)
    input_grad = whole_rows([by_y[0]] + [shift(by_y[j], "y", 4, j) for j in (1, 2, 3)])
    pair_own_b = dot(rows[:, :512], gu_b, ((0,), (0,)))
    down_own_a = dot(hid_all_a, cotan[:, :512], ((0,), (0,)))
    down_own_b = dot(hid_all_b, cotan[:, :512], ((0,), (0,)))
    wa, wb = SPLIT, 896 - SPLIT
    return (
        input_grad,
        final_add((pair_own_a[:, :wa], pair_own_b[:, :wb]), (pair_got_a[:, :wa], gate_got_b), 1),
        final_add((pair_own_a[:, wa:], pair_own_b[:, wb:]), (pair_got_a[:, wa:], up_got_b), 1),
        final_add((down_own_a, down_own_b), (down_got_a, down_got_b), 0),
    )


def solution(mesh):
    split = Mesh(mesh.devices.reshape(4, 2, 4, 2, 2), ("y", "z_hi", "x", "z_lo", "core"))
    fsdp, tsp = ("y", "z_hi"), ("x", "z_lo", "core")
    rows = P(fsdp + tsp, None)
    in_specs = (rows, rows, P(fsdp, tsp), P(fsdp, tsp), P(tsp, fsdp))
    out_specs = (rows, P(fsdp, tsp), P(fsdp, tsp), P(tsp, fsdp))
    return jax.shard_map(local, mesh=split, in_specs=in_specs, out_specs=out_specs, check_vma=False)
```

```python
import jax
import jax.numpy as jnp
from jax import lax
from jax.experimental import pallas as pl
from jax.experimental.pallas import tpu as pltpu
from jax.sharding import Mesh, PartitionSpec as P

BF = jnp.bfloat16
F32 = jnp.float32
SPLIT = 384
LIMIT = 20 * 1024 * 1024


def shift(value, axis, size, by):
    return lax.ppermute(value, axis, [(i, (i + by) % size) for i in range(size)])


def swap(value, axis):
    return shift(value, axis, 2, 1)


def after(value, *earlier):
    return lax.optimization_barrier((value,) + earlier)[0]


def dot(left, right, dims):
    return lax.dot_general(left, right, (dims, ((), ())), preferred_element_type=F32)


def kernel_call(body, shapes, *operands):
    spec = pl.BlockSpec(memory_space=pltpu.VMEM)
    return pl.pallas_call(
        body,
        out_shape=[jax.ShapeDtypeStruct(shape, kind) for shape, kind in shapes],
        in_specs=[spec] * len(operands),
        out_specs=[spec] * len(shapes),
        compiler_params=pltpu.CompilerParams(vmem_limit_bytes=LIMIT),
        cost_estimate=pl.CostEstimate(flops=0, bytes_accessed=0, transcendentals=0),
    )(*operands)


def feature_groups(pieces):
    def body(*refs):
        y, z_hi = lax.axis_index("y"), lax.axis_index("z_hi")
        for k in range(4):
            for half in range(2):
                at = pl.multiple_of(lax.rem(y + k, 4) * 1024 + lax.rem(z_hi + half, 2) * 512, 512)
                for i in range(len(pieces)):
                    refs[len(pieces) + k][i * 16 : (i + 1) * 16, half * 512 : (half + 1) * 512] = refs[i][
                        :, pl.ds(at, 512)
                    ]

    return kernel_call(body, [((16 * len(pieces), 1024), BF)] * 4, *pieces)


def whole_rows(groups):
    def body(*refs):
        y, z_hi = lax.axis_index("y"), lax.axis_index("z_hi")
        for k in range(4):
            for half in range(2):
                at = pl.multiple_of(lax.rem(y + 4 - k, 4) * 1024 + lax.rem(z_hi + half, 2) * 512, 512)
                refs[4][:, pl.ds(at, 512)] = refs[k][:, half * 512 : (half + 1) * 512]

    return kernel_call(body, [((16, 4096), BF)], *groups)[0]


def stack_rows(parts):
    def body(*refs):
        for y in range(4):
            refs[4][y * 32 : (y + 1) * 32] = refs[y][...]

    return kernel_call(body, [((128, 1024), BF)], *parts)[0]


def join_rows(mine, other):
    def body(mine_ref, other_ref, out_ref):
        out_ref[:128] = mine_ref[...]
        out_ref[128:] = other_ref[...]

    return kernel_call(body, [((256, 1024), BF)], mine, other)[0]


def assemble(own, other):
    def body(*refs):
        for core in range(2):
            for x in range(4):
                for z in range(2):
                    for y in range(4):
                        for which in range(2):
                            to = y * 256 + core * 128 + x * 32 + z * 16
                            at = z * 128 + y * 32 + which * 16
                            refs[8 + which][to : to + 16] = refs[4 * core + x][at : at + 16]

    return kernel_call(body, [((1024, 1024), BF)] * 2, *own, *other)


def forward(groups):
    plan, flat, total = [], [], 0
    for rows, turned, weights in groups:
        at = len(flat)
        flat.append(rows)
        for pair in weights:
            width = pair[0].shape[0 if turned else 1]
            plan.append((at, len(flat), turned, total, total + width))
            flat.extend(pair)
            total += width

    def body(*refs):
        own, up, down, low, high = refs[len(flat) :]
        for rows_at, pair_at, turned, start, stop in plan:
            cols = slice(start, stop)
            dims = (((1,), (1,)), ((), ())) if turned else (((1,), (0,)), ((), ()))
            for block in (2, 1, 3, 0):
                at = refs[rows_at][block * 256 : (block + 1) * 256]
                out = lax.dot_general(at[:, :512], refs[pair_at][...], dims, preferred_element_type=F32)
                out += lax.dot_general(at[:, 512:], refs[pair_at + 1][...], dims, preferred_element_type=F32)
                out = out.astype(BF)
                if block == 0:
                    own[:, cols] = out
                elif block == 1:
                    low[:, cols] = out[:128]
                    up[128:, cols] = out[128:]
                elif block == 2:
                    up[:128, cols] = out[:128]
                    down[:128, cols] = out[128:]
                else:
                    down[128:, cols] = out[:128]
                    high[:, cols] = out[128:]

    shapes = [((n, total), BF) for n in (256, 256, 256, 128, 128)]
    return kernel_call(body, shapes, *flat)


def add(left, right):
    return (left.astype(F32) + right.astype(F32)).astype(BF)


def ring_first(terms, axis="y"):
    return shift(terms[1], axis, 4, 1), shift(terms[2], axis, 4, -1)


def ring_second(terms, first, axis="y"):
    half = terms[3].shape[0]
    up, down = add(terms[3], first[0][:half]), add(terms[4], first[1][:half])
    return shift(up, axis, 4, 1), shift(down, axis, 4, -1)


def ring_sum(terms, first, second):
    own, half = terms[0].astype(F32), terms[3].shape[0]
    low = own[:half] + first[1][half:].astype(F32) + second[0].astype(F32)
    high = own[half:] + first[0][half:].astype(F32) + second[1].astype(F32)
    return jnp.concatenate([low, high])


def spread_first(own):
    return shift(own, "y", 4, 1), shift(own, "y", 4, -1)


def spread_second(first):
    return shift(first[0][:128], "y", 4, 1), shift(first[1][128:], "y", 4, -1)


def spread_all(own, first, second):
    return jnp.concatenate([own, first[1], second[0], second[1], first[0]])


def split_core(parts):
    def body(*refs):
        for half in range(2):
            cols = slice(half * 512, (half + 1) * 512)
            for y in range(4):
                for core in range(2):
                    at = slice(y * 256 + core * 128, y * 256 + core * 128 + 128)
                    total = refs[half][at]
                    for i in range(2 + half, len(parts), 2):
                        total += refs[i][at]
                    refs[len(parts) + core][y * 128 : (y + 1) * 128, cols] = total.astype(BF)

    return kernel_call(body, [((512, 1024), BF)] * 2, *parts)


def sum_core(keep, got):
    def body(*refs):
        own, up, down, low, high = refs[2:]
        for y in range(4):
            for x in range(4):
                at = slice((y * 4 + x) * 32, (y * 4 + x + 1) * 32)
                total = (refs[0][at].astype(F32) + refs[1][at].astype(F32)).astype(BF)
                half = slice(y % 2 * 32, y % 2 * 32 + 32)
                first = y < 2
                if x == 0:
                    own[y * 32 : (y + 1) * 32] = total
                elif x == 1:
                    (low if first else up.at[64:])[half] = total
                elif x == 2:
                    (up if first else down)[half] = total
                else:
                    (down.at[64:] if first else high)[half] = total

    return kernel_call(body, [((n, 1024), BF) for n in (128, 128, 128, 64, 64)], keep, got)


def sum_x(terms, first, second):
    def body(own, up, down, low, high, keep, send):
        for y in range(4):
            half = y % 2 * 32
            for z, out in enumerate((keep, send)):
                at = slice(half + z * 16, half + z * 16 + 16)
                far = slice(64 + half + z * 16, 64 + half + z * 16 + 16)
                total = own[y * 32 + z * 16 : y * 32 + z * 16 + 16].astype(F32)
                total += (down if y < 2 else up)[far].astype(F32)
                total += (low if y < 2 else high)[at].astype(F32)
                out[y * 16 : (y + 1) * 16] = total.astype(BF)

    return kernel_call(body, [((64, 1024), BF)] * 2, terms[0], *first, *second)


def add_to_rows(keep, got):
    def body(*refs):
        for y in range(4):
            at = slice(y * 16, (y + 1) * 16)
            refs[2 + y][...] = (refs[0][at].astype(F32) + refs[1][at].astype(F32)).astype(BF)

    return kernel_call(body, [((16, 1024), BF)] * 4, keep, got)


def final_add(own, other):
    def body(*refs):
        start = 0
        for ref in refs[1:-1]:
            at = slice(start, start + ref.shape[0])
            refs[-1][at] = refs[0][at] + ref[...].astype(F32)
            start += ref.shape[0]

    return kernel_call(body, [(own[0].shape, F32)], *own, *other)[0]


def together(first, *earlier):
    first = tuple(first)
    return lax.optimization_barrier(first + earlier)[: len(first)]


def input_terms(pgrad, weight, other_a, other_b):
    other = dot(pgrad[:, :SPLIT], other_a, ((1,), (1,))) + dot(pgrad[:, SPLIT:], other_b, ((1,), (1,)))
    return [dot(pgrad, weight, ((1,), (1,))), other]


def local(tokens, out_grad, gate_weight, up_weight, down_weight):
    gate = gate_weight[:, :SPLIT], gate_weight[:, SPLIT:]
    gate_a = swap(gate[0], "z_hi")
    groups = feature_groups([tokens, out_grad])
    mine = stack_rows([groups[0]] + [shift(groups[4 - j], "y", 4, -j) for j in (1, 2, 3)])
    mine = after(mine, gate_a)
    other = swap(mine, "z_lo")
    gate_b = swap(after(gate[1], other), "z_hi")
    down = down_weight[:SPLIT], down_weight[SPLIT:]
    down_a = swap(after(down[0], other), "z_hi")
    mine = join_rows(mine, other)
    own = [mine] + [shift(mine, "x", 4, -j) for j in (1, 2, 3)]
    own = together(own, gate_b, down_a)
    down_b = swap(after(down[1], gate_b), "z_hi")
    up_other = swap(after(up_weight, down_a), "z_hi")
    rows, cotan = assemble(own, [swap(piece, "core") for piece in own])

    gate_terms = forward([(rows, False, [(gate[0], gate_a), (gate[1], gate_b)])])
    gate_first = ring_first(gate_terms)
    cotan, down_b = together((cotan, down_b), *gate_first)
    grad_terms = forward([(cotan, True, [(down[0], down_a), (down[1], down_b)])])
    grad_first = ring_first(grad_terms)
    gate_second = ring_second(gate_terms, gate_first)
    up_terms = forward([(after(rows, *grad_first), False, [(up_weight, up_other)])])
    grad_second = ring_second(grad_terms, grad_first)
    up_first = ring_first(up_terms)
    gate_pre = ring_sum(gate_terms, gate_first, gate_second)
    sigmoid_gate = jax.nn.sigmoid(gate_pre)
    activated = gate_pre * sigmoid_gate
    hidden_grad = ring_sum(grad_terms, grad_first, grad_second)

    up_pgrad = (hidden_grad * activated).astype(BF)
    spread_up = spread_first(up_pgrad)
    up_first = together(up_first, *spread_up)
    up_second = ring_second(up_terms, up_first)
    up_pre = ring_sum(up_terms, up_first, up_second)
    gate_pgrad = hidden_grad * up_pre * sigmoid_gate * (1.0 + gate_pre * (1.0 - sigmoid_gate))
    gate_pgrad = gate_pgrad.astype(BF)
    hidden = (activated * up_pre).astype(BF)
    far_up = spread_second(spread_up)
    spread_gate = spread_first(gate_pgrad)
    far_up = together(far_up, gate_pgrad)
    up_all = spread_all(up_pgrad, spread_up, far_up)
    up_far = dot(rows[:, 512:], up_all, ((0,), (0,))).astype(BF)
    up_got = [swap(up_far, "z_hi")]
    spread_gate = together(spread_gate, up_far)
    far_gate = spread_second(spread_gate)
    spread_hid = spread_first(after(hidden, *far_gate))
    input_up = [dot(up_all, up_weight, ((1,), (1,))), dot(up_all, up_other, ((1,), (1,)))]
    gate_all = spread_all(gate_pgrad, spread_gate, far_gate)
    gate_far = dot(rows[:, 512:], gate_all, ((0,), (0,))).astype(BF)
    gate_got = [swap(gate_far[:320], "z_hi")]
    gate_all = after(gate_all, gate_far)

    input_gate = input_terms(gate_all, gate_weight, gate_a, gate_b)
    input_gate[0] = after(input_gate[0], *up_got)
    keep, send = split_core(input_up + input_gate)
    send = swap(send, "core")
    by_x = sum_core(keep, send)
    first = ring_first(by_x, "x")
    first = together(first, gate_got[0])
    gate_got.append(swap(after(gate_far[320:], up_got[0]), "z_hi"))
    spread_hid = together(spread_hid, *first)
    far_hid = spread_second(spread_hid)
    second = ring_second(by_x, first, "x")
    second = together(second, gate_got[1], *far_hid)
    keep, send = sum_x(by_x, first, second)
    got_z = swap(send, "z_lo")
    hid_all = spread_all(hidden, spread_hid, far_hid)
    down_far = dot(hid_all, cotan[:, 512:], ((0,), (0,))).astype(BF)
    down_got = [swap(after(down_far, got_z), "z_hi")]
    by_y = add_to_rows(keep, got_z)
    input_grad = whole_rows([by_y[0]] + [shift(by_y[j], "y", 4, j) for j in (1, 2, 3)])
    gate_own = dot(rows[:, :512], gate_all, ((0,), (0,)))
    up_own = dot(rows[:, :512], up_all, ((0,), (0,)))
    down_own = dot(hid_all, cotan[:, :512], ((0,), (0,)))
    return (
        input_grad,
        final_add([gate_own], gate_got),
        final_add([up_own], up_got),
        final_add([down_own], down_got),
    )


def solution(mesh):
    split = Mesh(mesh.devices.reshape(4, 2, 4, 2, 2), ("y", "z_hi", "x", "z_lo", "core"))
    fsdp, tsp = ("y", "z_hi"), ("x", "z_lo", "core")
    rows = P(fsdp + tsp, None)
    in_specs = (rows, rows, P(fsdp, tsp), P(fsdp, tsp), P(tsp, fsdp))
    out_specs = (rows, P(fsdp, tsp), P(fsdp, tsp), P(tsp, fsdp))
    return jax.shard_map(local, mesh=split, in_specs=in_specs, out_specs=out_specs, check_vma=False)
```

```python
import jax
import jax.numpy as jnp
from jax import lax
from jax.experimental import pallas as pl
from jax.experimental.pallas import tpu as pltpu
from jax.sharding import Mesh, PartitionSpec as P

BF = jnp.bfloat16
F32 = jnp.float32
SPLIT = 384
LIMIT = 20 * 1024 * 1024


def shift(value, axis, size, by):
    return lax.ppermute(value, axis, [(i, (i + by) % size) for i in range(size)])


def swap(value, axis):
    return shift(value, axis, 2, 1)


def after(value, *earlier):
    return lax.optimization_barrier((value,) + earlier)[0]


def dot(left, right, dims):
    return lax.dot_general(left, right, (dims, ((), ())), preferred_element_type=F32)


def kernel_call(body, shapes, *operands):
    spec = pl.BlockSpec(memory_space=pltpu.VMEM)
    return pl.pallas_call(
        body,
        out_shape=[jax.ShapeDtypeStruct(shape, kind) for shape, kind in shapes],
        in_specs=[spec] * len(operands),
        out_specs=[spec] * len(shapes),
        compiler_params=pltpu.CompilerParams(vmem_limit_bytes=LIMIT),
        cost_estimate=pl.CostEstimate(flops=0, bytes_accessed=0, transcendentals=0),
    )(*operands)


def feature_groups(pieces):
    count = len(pieces)

    def body(*refs):
        held, sems = refs[count + 4 : -1], refs[-1]
        copies = [pltpu.make_async_copy(refs[i], held[i], sems.at[i]) for i in range(count)]
        for copy in copies:
            copy.start()
        y, z_hi = lax.axis_index("y"), lax.axis_index("z_hi")
        for i in range(count):
            copies[i].wait()
            for k in range(4):
                for half in range(2):
                    at = pl.multiple_of(lax.rem(y + k, 4) * 1024 + lax.rem(z_hi + half, 2) * 512, 512)
                    refs[count + k][i * 16 : (i + 1) * 16, half * 512 : (half + 1) * 512] = held[i][:, pl.ds(at, 512)]

    return pl.pallas_call(
        body,
        out_shape=[jax.ShapeDtypeStruct((16 * count, 1024), BF)] * 4,
        in_specs=[pl.BlockSpec(memory_space=pl.ANY)] * count,
        out_specs=[pl.BlockSpec(memory_space=pltpu.VMEM)] * 4,
        scratch_shapes=[pltpu.VMEM((16, 4096), BF)] * count + [pltpu.SemaphoreType.DMA((count,))],
        compiler_params=pltpu.CompilerParams(vmem_limit_bytes=LIMIT),
        cost_estimate=pl.CostEstimate(flops=0, bytes_accessed=0, transcendentals=0),
    )(*pieces)


def whole_rows(groups):
    def body(*refs):
        y, z_hi = lax.axis_index("y"), lax.axis_index("z_hi")
        for k in range(4):
            for half in range(2):
                at = pl.multiple_of(lax.rem(y + 4 - k, 4) * 1024 + lax.rem(z_hi + half, 2) * 512, 512)
                refs[4][:, pl.ds(at, 512)] = refs[k][:, half * 512 : (half + 1) * 512]

    return kernel_call(body, [((16, 4096), BF)], *groups)[0]


def stack_rows(parts):
    def body(*refs):
        for y in range(4):
            refs[4][y * 32 : (y + 1) * 32] = refs[y][...]

    return kernel_call(body, [((128, 1024), BF)], *parts)[0]


def join_rows(mine, other):
    def body(mine_ref, other_ref, out_ref):
        out_ref[:128] = mine_ref[...]
        out_ref[128:] = other_ref[...]

    return kernel_call(body, [((256, 1024), BF)], mine, other)[0]


def join_x(own, first, second):
    def body(own_ref, minus, plus, low, high, *outs):
        for y in range(4):
            for x, ref in enumerate((own_ref, plus, None, minus)):
                for z in range(2):
                    for which in range(2):
                        to = (y * 4 + x) * 32 + z * 16
                        at = y * 32 + which * 16
                        if x == 2:
                            outs[which][to : to + 16] = (high if z else low)[at : at + 16]
                        else:
                            outs[which][to : to + 16] = ref[z * 128 + at : z * 128 + at + 16]

    return kernel_call(body, [((512, 1024), BF)] * 2, own, *first, *second)


def join_core(own, other):
    def body(own_ref, other_ref, out):
        for y in range(4):
            out[y * 256 : y * 256 + 128] = own_ref[y * 128 : (y + 1) * 128]
            out[y * 256 + 128 : (y + 1) * 256] = other_ref[y * 128 : (y + 1) * 128]

    return kernel_call(body, [((1024, 1024), BF)], own, other)[0]


def forward(groups):
    plan, flat, total = [], [], 0
    for rows, turned, weights in groups:
        at = len(flat)
        flat.append(rows)
        for pair in weights:
            width = pair[0].shape[0 if turned else 1]
            plan.append((at, len(flat), turned, total, total + width))
            flat.extend(pair)
            total += width

    def body(*refs):
        own, up, down, low, high = refs[len(flat) :]
        for rows_at, pair_at, turned, start, stop in plan:
            cols = slice(start, stop)
            dims = (((1,), (1,)), ((), ())) if turned else (((1,), (0,)), ((), ()))
            for block in (2, 1, 3, 0):
                at = refs[rows_at][block * 256 : (block + 1) * 256]
                out = lax.dot_general(at[:, :512], refs[pair_at][...], dims, preferred_element_type=F32)
                out += lax.dot_general(at[:, 512:], refs[pair_at + 1][...], dims, preferred_element_type=F32)
                out = out.astype(BF)
                if block == 0:
                    own[:, cols] = out
                elif block == 1:
                    low[:, cols] = out[:128]
                    up[128:, cols] = out[128:]
                elif block == 2:
                    up[:128, cols] = out[:128]
                    down[:128, cols] = out[128:]
                else:
                    down[128:, cols] = out[:128]
                    high[:, cols] = out[128:]

    shapes = [((n, total), BF) for n in (256, 256, 256, 128, 128)]
    return kernel_call(body, shapes, *flat)


def add(left, right):
    return (left.astype(F32) + right.astype(F32)).astype(BF)


def ring_first(terms, axis="y"):
    return shift(terms[1], axis, 4, 1), shift(terms[2], axis, 4, -1)


def ring_second(terms, first, axis="y"):
    half = terms[3].shape[0]
    up, down = add(terms[3], first[0][:half]), add(terms[4], first[1][:half])
    return shift(up, axis, 4, 1), shift(down, axis, 4, -1)


def ring_sum(terms, first, second):
    own, half = terms[0].astype(F32), terms[3].shape[0]
    low = own[:half] + first[1][half:].astype(F32) + second[0].astype(F32)
    high = own[half:] + first[0][half:].astype(F32) + second[1].astype(F32)
    return jnp.concatenate([low, high])


def spread_first(own, axis="y"):
    return shift(own, axis, 4, 1), shift(own, axis, 4, -1)


def spread_second(first, axis="y"):
    half = first[0].shape[0] // 2
    return shift(first[0][:half], axis, 4, 1), shift(first[1][half:], axis, 4, -1)


def spread_all(own, first, second):
    return jnp.concatenate([own, first[1], second[0], second[1], first[0]])


def split_core(parts):
    def body(*refs):
        for half in range(2):
            cols = slice(half * 512, (half + 1) * 512)
            for y in range(4):
                for core in range(2):
                    at = slice(y * 256 + core * 128, y * 256 + core * 128 + 128)
                    total = refs[half][at]
                    for i in range(2 + half, len(parts), 2):
                        total += refs[i][at]
                    refs[len(parts) + core][y * 128 : (y + 1) * 128, cols] = total.astype(BF)

    return kernel_call(body, [((512, 1024), BF)] * 2, *parts)


def sum_core(keep, got):
    def body(*refs):
        own, up, down, low, high = refs[2:]
        for y in range(4):
            for x in range(4):
                at = slice((y * 4 + x) * 32, (y * 4 + x + 1) * 32)
                total = (refs[0][at].astype(F32) + refs[1][at].astype(F32)).astype(BF)
                half = slice(y % 2 * 32, y % 2 * 32 + 32)
                first = y < 2
                if x == 0:
                    own[y * 32 : (y + 1) * 32] = total
                elif x == 1:
                    (low if first else up.at[64:])[half] = total
                elif x == 2:
                    (up if first else down)[half] = total
                else:
                    (down.at[64:] if first else high)[half] = total

    return kernel_call(body, [((n, 1024), BF) for n in (128, 128, 128, 64, 64)], keep, got)


def sum_x(terms, first, second):
    def body(own, up, down, low, high, keep, send):
        for y in range(4):
            half = y % 2 * 32
            for z, out in enumerate((keep, send)):
                at = slice(half + z * 16, half + z * 16 + 16)
                far = slice(64 + half + z * 16, 64 + half + z * 16 + 16)
                total = own[y * 32 + z * 16 : y * 32 + z * 16 + 16].astype(F32)
                total += (down if y < 2 else up)[far].astype(F32)
                total += (low if y < 2 else high)[at].astype(F32)
                out[y * 16 : (y + 1) * 16] = total.astype(BF)

    return kernel_call(body, [((64, 1024), BF)] * 2, terms[0], *first, *second)


def add_to_rows(keep, got):
    def body(*refs):
        for y in range(4):
            at = slice(y * 16, (y + 1) * 16)
            refs[2 + y][...] = (refs[0][at].astype(F32) + refs[1][at].astype(F32)).astype(BF)

    return kernel_call(body, [((16, 1024), BF)] * 4, keep, got)


def final_add(own, other):
    def body(*refs):
        start = 0
        for ref in refs[1:-1]:
            at = slice(start, start + ref.shape[0])
            refs[-1][at] = refs[0][at] + ref[...].astype(F32)
            start += ref.shape[0]

    return kernel_call(body, [(own[0].shape, F32)], *own, *other)[0]


def together(first, *earlier):
    first = tuple(first)
    return lax.optimization_barrier(first + earlier)[: len(first)]


def input_terms(pgrad, weight, other_a, other_b):
    other = dot(pgrad[:, :SPLIT], other_a, ((1,), (1,))) + dot(pgrad[:, SPLIT:], other_b, ((1,), (1,)))
    return [dot(pgrad, weight, ((1,), (1,))), other]


def local(tokens, out_grad, gate_weight, up_weight, down_weight):
    gate = gate_weight[:, :SPLIT], gate_weight[:, SPLIT:]
    gate_a = swap(gate[0], "z_hi")
    groups = feature_groups([tokens, out_grad])
    mine = stack_rows([groups[0]] + [shift(groups[4 - j], "y", 4, -j) for j in (1, 2, 3)])
    mine = after(mine, gate_a)
    other = swap(mine, "z_lo")
    gate_b = swap(after(gate[1], other), "z_hi")
    down = down_weight[:256], down_weight[256:640], down_weight[640:]
    down_a = swap(after(down[0], other), "z_hi")
    mine = join_rows(mine, other)
    x_first = together(spread_first(mine, "x"), gate_b)
    down_b = swap(after(down[1], gate_b), "z_hi")
    x_second = together(spread_second(x_first, "x"), down_a, down_b)
    tok, cot = join_x(mine, x_first, x_second)
    down_c = swap(after(down[2], down_a), "z_hi")
    rows = join_core(tok, swap(tok, "core"))
    cotan = join_core(cot, swap(cot, "core"))
    up_other = swap(after(up_weight, down_b), "z_hi")

    gate_terms = forward([(rows, False, [(gate[0], gate_a), (gate[1], gate_b)])])
    gate_first = ring_first(gate_terms)
    cotan = after(cotan, gate_terms[0])
    grad_terms = forward([(cotan, True, list(zip(down, (down_a, down_b, down_c))))])
    grad_first = ring_first(grad_terms)
    gate_second = ring_second(gate_terms, gate_first)
    up_terms = forward([(after(rows, grad_terms[0], *gate_first), False, [(up_weight, up_other)])])
    grad_second = ring_second(grad_terms, grad_first)
    up_first = ring_first(up_terms)
    gate_pre = ring_sum(gate_terms, gate_first, gate_second)
    sigmoid_gate = jax.nn.sigmoid(gate_pre)
    activated = gate_pre * sigmoid_gate
    hidden_grad = ring_sum(grad_terms, grad_first, grad_second)

    up_pgrad = (hidden_grad * activated).astype(BF)
    spread_up = spread_first(up_pgrad)
    up_first = together(up_first, *spread_up)
    up_second = ring_second(up_terms, up_first)
    up_pre = ring_sum(up_terms, up_first, up_second)
    gate_pgrad = hidden_grad * up_pre * sigmoid_gate * (1.0 + gate_pre * (1.0 - sigmoid_gate))
    gate_pgrad = gate_pgrad.astype(BF)
    hidden = (activated * up_pre).astype(BF)
    far_up = spread_second(spread_up)
    spread_gate = spread_first(gate_pgrad)
    far_up = together(far_up, gate_pgrad)
    up_all = spread_all(up_pgrad, spread_up, far_up)
    up_far = dot(rows[:, 512:], up_all, ((0,), (0,))).astype(BF)
    up_got = [swap(up_far, "z_hi")]
    spread_gate = together(spread_gate, up_far)
    far_gate = spread_second(spread_gate)
    spread_hid = spread_first(after(hidden, *far_gate))
    input_up = [dot(up_all, up_weight, ((1,), (1,))), dot(up_all, up_other, ((1,), (1,)))]
    gate_all = spread_all(gate_pgrad, spread_gate, far_gate)
    gate_far = dot(rows[:, 512:], gate_all, ((0,), (0,))).astype(BF)
    gate_got = [swap(gate_far[:256], "z_hi")]
    gate_all = after(gate_all, gate_far)

    input_gate = input_terms(gate_all, gate_weight, gate_a, gate_b)
    input_gate[0] = after(input_gate[0], *up_got)
    keep, send = split_core(input_up + input_gate)
    send = swap(send, "core")
    by_x = sum_core(keep, send)
    first = ring_first(by_x, "x")
    first = together(first, gate_got[0])
    gate_got.append(swap(after(gate_far[256:], up_got[0]), "z_hi"))
    far_hid = spread_second(together(spread_hid, first[0]))
    second = ring_second(by_x, first, "x")
    second = together(second, gate_got[1], *far_hid)
    keep, send = sum_x(by_x, first, second)
    hid_all = spread_all(hidden, spread_hid, far_hid)
    down_far = dot(hid_all, cotan[:, 512:], ((0,), (0,))).astype(BF)
    got_z = swap(send, "z_lo")
    down_got = [swap(down_far, "z_hi")]
    by_y = add_to_rows(keep, got_z)
    input_grad = whole_rows([by_y[0]] + [shift(by_y[j], "y", 4, j) for j in (1, 2, 3)])
    rows_own = after(rows[:, :512], by_y[0])
    gate_own = dot(rows_own, gate_all, ((0,), (0,)))
    up_own = dot(rows_own, up_all, ((0,), (0,)))
    down_own = dot(hid_all, cotan[:, :512], ((0,), (0,)))
    return (
        input_grad,
        final_add([gate_own], gate_got),
        final_add([up_own], up_got),
        final_add([down_own], down_got),
    )


def solution(mesh):
    split = Mesh(mesh.devices.reshape(4, 2, 4, 2, 2), ("y", "z_hi", "x", "z_lo", "core"))
    fsdp, tsp = ("y", "z_hi"), ("x", "z_lo", "core")
    rows = P(fsdp + tsp, None)
    in_specs = (rows, rows, P(fsdp, tsp), P(fsdp, tsp), P(tsp, fsdp))
    out_specs = (rows, P(fsdp, tsp), P(fsdp, tsp), P(tsp, fsdp))
    return jax.shard_map(local, mesh=split, in_specs=in_specs, out_specs=out_specs, check_vma=False)
```

```python
import jax
import jax.numpy as jnp
from jax import lax
from jax.experimental import pallas as pl
from jax.experimental.pallas import tpu as pltpu
from jax.sharding import Mesh, PartitionSpec as P

BF = jnp.bfloat16
F32 = jnp.float32
SPLIT = 384
LIMIT = 20 * 1024 * 1024


def shift(value, axis, size, by):
    return lax.ppermute(value, axis, [(i, (i + by) % size) for i in range(size)])


def swap(value, axis):
    return shift(value, axis, 2, 1)


def after(value, *earlier):
    return lax.optimization_barrier((value,) + earlier)[0]


def dot(left, right, dims):
    return lax.dot_general(left, right, (dims, ((), ())), preferred_element_type=F32)


def kernel_call(body, shapes, *operands):
    spec = pl.BlockSpec(memory_space=pltpu.VMEM)
    return pl.pallas_call(
        body,
        out_shape=[jax.ShapeDtypeStruct(shape, kind) for shape, kind in shapes],
        in_specs=[spec] * len(operands),
        out_specs=[spec] * len(shapes),
        compiler_params=pltpu.CompilerParams(vmem_limit_bytes=LIMIT),
        cost_estimate=pl.CostEstimate(flops=0, bytes_accessed=0, transcendentals=0),
    )(*operands)


def feature_groups(pieces):
    count = len(pieces)

    def body(*refs):
        held, sems = refs[count + 4 : -1], refs[-1]
        copies = [pltpu.make_async_copy(refs[i], held[i], sems.at[i]) for i in range(count)]
        for copy in copies:
            copy.start()
        y, z_hi = lax.axis_index("y"), lax.axis_index("z_hi")
        for i in range(count):
            copies[i].wait()
            for k in range(4):
                for half in range(2):
                    at = pl.multiple_of(lax.rem(y + k, 4) * 1024 + lax.rem(z_hi + half, 2) * 512, 512)
                    refs[count + k][i * 16 : (i + 1) * 16, half * 512 : (half + 1) * 512] = held[i][:, pl.ds(at, 512)]

    return pl.pallas_call(
        body,
        out_shape=[jax.ShapeDtypeStruct((16 * count, 1024), BF)] * 4,
        in_specs=[pl.BlockSpec(memory_space=pl.ANY)] * count,
        out_specs=[pl.BlockSpec(memory_space=pltpu.VMEM)] * 4,
        scratch_shapes=[pltpu.VMEM((16, 4096), BF)] * count + [pltpu.SemaphoreType.DMA((count,))],
        compiler_params=pltpu.CompilerParams(vmem_limit_bytes=LIMIT),
        cost_estimate=pl.CostEstimate(flops=0, bytes_accessed=0, transcendentals=0),
    )(*pieces)


def whole_rows(groups):
    def body(*refs):
        y, z_hi = lax.axis_index("y"), lax.axis_index("z_hi")
        for k in range(4):
            for half in range(2):
                at = pl.multiple_of(lax.rem(y + 4 - k, 4) * 1024 + lax.rem(z_hi + half, 2) * 512, 512)
                refs[4][:, pl.ds(at, 512)] = refs[k][:, half * 512 : (half + 1) * 512]

    return kernel_call(body, [((16, 4096), BF)], *groups)[0]


def stack_rows(parts):
    def body(*refs):
        for y in range(4):
            refs[4][y * 32 : (y + 1) * 32] = refs[y][...]

    return kernel_call(body, [((128, 1024), BF)], *parts)[0]


def join_rows(mine, other):
    def body(mine_ref, other_ref, out_ref):
        out_ref[:128] = mine_ref[...]
        out_ref[128:] = other_ref[...]

    return kernel_call(body, [((256, 1024), BF)], mine, other)[0]


def join_x(own, first, second):
    def body(own_ref, minus, plus, low, high, *outs):
        for y in range(4):
            for x, ref in enumerate((own_ref, plus, None, minus)):
                for z in range(2):
                    for which in range(2):
                        to = (y * 4 + x) * 32 + z * 16
                        at = y * 32 + which * 16
                        if x == 2:
                            outs[which][to : to + 16] = (high if z else low)[at : at + 16]
                        else:
                            outs[which][to : to + 16] = ref[z * 128 + at : z * 128 + at + 16]

    return kernel_call(body, [((512, 1024), BF)] * 2, own, *first, *second)


def join_core(own, other):
    def body(own_ref, other_ref, out):
        for y in range(4):
            out[y * 256 : y * 256 + 128] = own_ref[y * 128 : (y + 1) * 128]
            out[y * 256 + 128 : (y + 1) * 256] = other_ref[y * 128 : (y + 1) * 128]

    return kernel_call(body, [((1024, 1024), BF)], own, other)[0]


def forward(groups):
    plan, flat, total = [], [], 0
    for rows, turned, weights in groups:
        at = len(flat)
        flat.append(rows)
        for pair in weights:
            width = pair[0].shape[0 if turned else 1]
            plan.append((at, len(flat), turned, total, total + width))
            flat.extend(pair)
            total += width

    def body(*refs):
        own, up, down, low, high = refs[len(flat) :]
        for rows_at, pair_at, turned, start, stop in plan:
            cols = slice(start, stop)
            dims = (((1,), (1,)), ((), ())) if turned else (((1,), (0,)), ((), ()))
            for block in (2, 1, 3, 0):
                at = refs[rows_at][block * 256 : (block + 1) * 256]
                out = lax.dot_general(at[:, :512], refs[pair_at][...], dims, preferred_element_type=F32)
                out += lax.dot_general(at[:, 512:], refs[pair_at + 1][...], dims, preferred_element_type=F32)
                out = out.astype(BF)
                if block == 0:
                    own[:, cols] = out
                elif block == 1:
                    low[:, cols] = out[:128]
                    up[128:, cols] = out[128:]
                elif block == 2:
                    up[:128, cols] = out[:128]
                    down[:128, cols] = out[128:]
                else:
                    down[128:, cols] = out[:128]
                    high[:, cols] = out[128:]

    shapes = [((n, total), BF) for n in (256, 256, 256, 128, 128)]
    return kernel_call(body, shapes, *flat)


def add(left, right):
    return (left.astype(F32) + right.astype(F32)).astype(BF)


def ring_first(terms, axis="y"):
    return shift(terms[1], axis, 4, 1), shift(terms[2], axis, 4, -1)


def ring_second(terms, first, axis="y"):
    half = terms[3].shape[0]
    up, down = add(terms[3], first[0][:half]), add(terms[4], first[1][:half])
    return shift(up, axis, 4, 1), shift(down, axis, 4, -1)


def ring_sum(terms, first, second):
    own, half = terms[0].astype(F32), terms[3].shape[0]
    low = own[:half] + first[1][half:].astype(F32) + second[0].astype(F32)
    high = own[half:] + first[0][half:].astype(F32) + second[1].astype(F32)
    return jnp.concatenate([low, high])


def spread_first(own, axis="y"):
    return shift(own, axis, 4, 1), shift(own, axis, 4, -1)


def spread_second(first, axis="y"):
    half = first[0].shape[0] // 2
    return shift(first[0][:half], axis, 4, 1), shift(first[1][half:], axis, 4, -1)


def spread_all(own, first, second):
    return jnp.concatenate([own, first[1], second[0], second[1], first[0]])


def split_core(parts):
    def body(*refs):
        for half in range(2):
            cols = slice(half * 512, (half + 1) * 512)
            for y in range(4):
                for core in range(2):
                    at = slice(y * 256 + core * 128, y * 256 + core * 128 + 128)
                    total = refs[half][at]
                    for i in range(2 + half, len(parts), 2):
                        total += refs[i][at]
                    refs[len(parts) + core][y * 128 : (y + 1) * 128, cols] = total.astype(BF)

    return kernel_call(body, [((512, 1024), BF)] * 2, *parts)


def sum_core(keep, got):
    def body(*refs):
        own, up, down, low, high = refs[2:]
        for y in range(4):
            for x in range(4):
                at = slice((y * 4 + x) * 32, (y * 4 + x + 1) * 32)
                total = (refs[0][at].astype(F32) + refs[1][at].astype(F32)).astype(BF)
                half = slice(y % 2 * 32, y % 2 * 32 + 32)
                first = y < 2
                if x == 0:
                    own[y * 32 : (y + 1) * 32] = total
                elif x == 1:
                    (low if first else up.at[64:])[half] = total
                elif x == 2:
                    (up if first else down)[half] = total
                else:
                    (down.at[64:] if first else high)[half] = total

    return kernel_call(body, [((n, 1024), BF) for n in (128, 128, 128, 64, 64)], keep, got)


def sum_x(terms, first, second):
    def body(own, up, down, low, high, keep, send):
        for y in range(4):
            half = y % 2 * 32
            for z, out in enumerate((keep, send)):
                at = slice(half + z * 16, half + z * 16 + 16)
                far = slice(64 + half + z * 16, 64 + half + z * 16 + 16)
                total = own[y * 32 + z * 16 : y * 32 + z * 16 + 16].astype(F32)
                total += (down if y < 2 else up)[far].astype(F32)
                total += (low if y < 2 else high)[at].astype(F32)
                out[y * 16 : (y + 1) * 16] = total.astype(BF)

    return kernel_call(body, [((64, 1024), BF)] * 2, terms[0], *first, *second)


def add_to_rows(keep, got):
    def body(*refs):
        for y in range(4):
            at = slice(y * 16, (y + 1) * 16)
            refs[2 + y][...] = (refs[0][at].astype(F32) + refs[1][at].astype(F32)).astype(BF)

    return kernel_call(body, [((16, 1024), BF)] * 4, keep, got)


def final_add(own, other):
    def body(*refs):
        start = 0
        for ref in refs[1:-1]:
            at = slice(start, start + ref.shape[0])
            refs[-1][at] = refs[0][at] + ref[...].astype(F32)
            start += ref.shape[0]

    return kernel_call(body, [(own[0].shape, F32)], *own, *other)[0]


def together(first, *earlier):
    first = tuple(first)
    return lax.optimization_barrier(first + earlier)[: len(first)]


def input_terms(pgrad, weight, other_a, other_b):
    other = dot(pgrad[:, :SPLIT], other_a, ((1,), (1,))) + dot(pgrad[:, SPLIT:], other_b, ((1,), (1,)))
    return [dot(pgrad, weight, ((1,), (1,))), other]


def local(tokens, out_grad, gate_weight, up_weight, down_weight):
    gate = gate_weight[:, :SPLIT], gate_weight[:, SPLIT:]
    gate_a = swap(gate[0], "z_hi")
    groups = feature_groups([tokens, out_grad])
    mine = stack_rows([groups[0]] + [shift(groups[4 - j], "y", 4, -j) for j in (1, 2, 3)])
    mine = after(mine, gate_a)
    other = swap(mine, "z_lo")
    gate_b = swap(after(gate[1], other), "z_hi")
    down = down_weight[:256], down_weight[256:640], down_weight[640:]
    down_a = swap(after(down[0], other), "z_hi")
    mine = join_rows(mine, other)
    x_first = together(spread_first(mine, "x"), gate_b)
    down_b = swap(after(down[1], gate_b), "z_hi")
    x_second = together(spread_second(x_first, "x"), down_a, down_b)
    tok, cot = join_x(mine, x_first, x_second)
    down_c = swap(after(down[2], down_a), "z_hi")
    rows = join_core(tok, swap(tok, "core"))
    cotan = join_core(cot, swap(cot, "core"))
    up_other = swap(after(up_weight, down_b), "z_hi")

    gate_terms = forward([(rows, False, [(gate[0], gate_a), (gate[1], gate_b)])])
    gate_first = ring_first(gate_terms)
    cotan = after(cotan, gate_terms[0])
    grad_terms = forward([(cotan, True, list(zip(down, (down_a, down_b, down_c))))])
    grad_first = ring_first(grad_terms)
    gate_second = ring_second(gate_terms, gate_first)
    up_terms = forward([(after(rows, grad_terms[0], *gate_first), False, [(up_weight, up_other)])])
    grad_second = ring_second(grad_terms, grad_first)
    up_first = ring_first(up_terms)
    gate_pre = ring_sum(gate_terms, gate_first, gate_second)
    sigmoid_gate = jax.nn.sigmoid(gate_pre)
    activated = gate_pre * sigmoid_gate
    hidden_grad = ring_sum(grad_terms, grad_first, grad_second)

    up_pgrad = (hidden_grad * activated).astype(BF)
    spread_up = spread_first(up_pgrad)
    up_first = together(up_first, *spread_up)
    up_second = ring_second(up_terms, up_first)
    up_pre = ring_sum(up_terms, up_first, up_second)
    gate_pgrad = hidden_grad * up_pre * sigmoid_gate * (1.0 + gate_pre * (1.0 - sigmoid_gate))
    gate_pgrad = gate_pgrad.astype(BF)
    hidden = (activated * up_pre).astype(BF)
    far_up = spread_second(spread_up)
    spread_gate = spread_first(gate_pgrad)
    far_up = together(far_up, gate_pgrad)
    up_all = spread_all(up_pgrad, spread_up, far_up)
    up_far = dot(rows[:, 512:], up_all, ((0,), (0,))).astype(BF)
    up_got = [swap(up_far, "z_hi")]
    spread_gate = together(spread_gate, up_far)
    far_gate = spread_second(spread_gate)
    spread_hid = spread_first(after(hidden, *far_gate))
    input_up = [dot(up_all, up_weight, ((1,), (1,))), dot(up_all, up_other, ((1,), (1,)))]
    gate_all = spread_all(gate_pgrad, spread_gate, far_gate)
    gate_far = dot(rows[:, 512:], gate_all, ((0,), (0,))).astype(BF)
    gate_got = [swap(gate_far, "z_hi")]
    gate_all = after(gate_all, gate_far)

    input_gate = input_terms(gate_all, gate_weight, gate_a, gate_b)
    input_gate[0] = after(input_gate[0], *up_got)
    keep, send = split_core(input_up + input_gate)
    send = swap(send, "core")
    by_x = sum_core(keep, send)
    first = ring_first(by_x, "x")
    far_hid = spread_second(together(spread_hid, first[0]))
    second = ring_second(by_x, first, "x")
    second = together(second, gate_got[0], *far_hid)
    keep, send = sum_x(by_x, first, second)
    hid_all = spread_all(hidden, spread_hid, far_hid)
    down_far = dot(hid_all, cotan[:, 512:], ((0,), (0,))).astype(BF)
    got_z = swap(send, "z_lo")
    down_got = [swap(down_far, "z_hi")]
    by_y = add_to_rows(keep, got_z)
    input_grad = whole_rows([by_y[0]] + [shift(by_y[j], "y", 4, j) for j in (1, 2, 3)])
    rows_own = after(rows[:, :512], by_y[0])
    gate_own = dot(rows_own, gate_all, ((0,), (0,)))
    up_own = dot(rows_own, up_all, ((0,), (0,)))
    down_own = dot(hid_all, cotan[:, :512], ((0,), (0,)))
    return (
        input_grad,
        final_add([gate_own], gate_got),
        final_add([up_own], up_got),
        final_add([down_own], down_got),
    )


def solution(mesh):
    split = Mesh(mesh.devices.reshape(4, 2, 4, 2, 2), ("y", "z_hi", "x", "z_lo", "core"))
    fsdp, tsp = ("y", "z_hi"), ("x", "z_lo", "core")
    rows = P(fsdp + tsp, None)
    in_specs = (rows, rows, P(fsdp, tsp), P(fsdp, tsp), P(tsp, fsdp))
    out_specs = (rows, P(fsdp, tsp), P(fsdp, tsp), P(tsp, fsdp))
    return jax.shard_map(local, mesh=split, in_specs=in_specs, out_specs=out_specs, check_vma=False)
```

```python
import jax
import jax.numpy as jnp
from jax import lax
from jax.experimental import pallas as pl
from jax.experimental.pallas import tpu as pltpu
from jax.sharding import Mesh, PartitionSpec as P

BF = jnp.bfloat16
F32 = jnp.float32
SPLIT = 384
LIMIT = 20 * 1024 * 1024


def shift(value, axis, size, by):
    return lax.ppermute(value, axis, [(i, (i + by) % size) for i in range(size)])


def swap(value, axis):
    return shift(value, axis, 2, 1)


def after(value, *earlier):
    return lax.optimization_barrier((value,) + earlier)[0]


def dot(left, right, dims):
    return lax.dot_general(left, right, (dims, ((), ())), preferred_element_type=F32)


def kernel_call(body, shapes, *operands):
    spec = pl.BlockSpec(memory_space=pltpu.VMEM)
    return pl.pallas_call(
        body,
        out_shape=[jax.ShapeDtypeStruct(shape, kind) for shape, kind in shapes],
        in_specs=[spec] * len(operands),
        out_specs=[spec] * len(shapes),
        compiler_params=pltpu.CompilerParams(vmem_limit_bytes=LIMIT),
        cost_estimate=pl.CostEstimate(flops=0, bytes_accessed=0, transcendentals=0),
    )(*operands)


def feature_groups(pieces):
    count = len(pieces)

    def body(*refs):
        held, sems = refs[count + 4 : -1], refs[-1]
        copies = [pltpu.make_async_copy(refs[i], held[i], sems.at[i]) for i in range(count)]
        for copy in copies:
            copy.start()
        y, z_hi = lax.axis_index("y"), lax.axis_index("z_hi")
        for i in range(count):
            copies[i].wait()
            for k in range(4):
                for half in range(2):
                    at = pl.multiple_of(lax.rem(y + k, 4) * 1024 + lax.rem(z_hi + half, 2) * 512, 512)
                    refs[count + k][i * 16 : (i + 1) * 16, half * 512 : (half + 1) * 512] = held[i][:, pl.ds(at, 512)]

    return pl.pallas_call(
        body,
        out_shape=[jax.ShapeDtypeStruct((16 * count, 1024), BF)] * 4,
        in_specs=[pl.BlockSpec(memory_space=pl.ANY)] * count,
        out_specs=[pl.BlockSpec(memory_space=pltpu.VMEM)] * 4,
        scratch_shapes=[pltpu.VMEM((16, 4096), BF)] * count + [pltpu.SemaphoreType.DMA((count,))],
        compiler_params=pltpu.CompilerParams(vmem_limit_bytes=LIMIT),
        cost_estimate=pl.CostEstimate(flops=0, bytes_accessed=0, transcendentals=0),
    )(*pieces)


def whole_rows(groups):
    def body(*refs):
        y, z_hi = lax.axis_index("y"), lax.axis_index("z_hi")
        for k in range(4):
            for half in range(2):
                at = pl.multiple_of(lax.rem(y + 4 - k, 4) * 1024 + lax.rem(z_hi + half, 2) * 512, 512)
                refs[4][:, pl.ds(at, 512)] = refs[k][:, half * 512 : (half + 1) * 512]

    return kernel_call(body, [((16, 4096), BF)], *groups)[0]


def stack_rows(parts):
    def body(*refs):
        for y in range(4):
            refs[4][y * 32 : (y + 1) * 32] = refs[y][...]

    return kernel_call(body, [((128, 1024), BF)], *parts)[0]


def join_rows(mine, other):
    def body(mine_ref, other_ref, out_ref):
        out_ref[:128] = mine_ref[...]
        out_ref[128:] = other_ref[...]

    return kernel_call(body, [((256, 1024), BF)], mine, other)[0]


def join_x(own, first, second):
    def body(own_ref, minus, plus, low, high, *outs):
        for y in range(4):
            for x, ref in enumerate((own_ref, plus, None, minus)):
                for z in range(2):
                    for which in range(2):
                        to = (y * 4 + x) * 32 + z * 16
                        at = y * 32 + which * 16
                        if x == 2:
                            outs[which][to : to + 16] = (high if z else low)[at : at + 16]
                        else:
                            outs[which][to : to + 16] = ref[z * 128 + at : z * 128 + at + 16]

    return kernel_call(body, [((512, 1024), BF)] * 2, own, *first, *second)


def join_core(own, other):
    def body(own_ref, other_ref, out):
        for y in range(4):
            out[y * 256 : y * 256 + 128] = own_ref[y * 128 : (y + 1) * 128]
            out[y * 256 + 128 : (y + 1) * 256] = other_ref[y * 128 : (y + 1) * 128]

    return kernel_call(body, [((1024, 1024), BF)], own, other)[0]


def forward(groups):
    plan, flat, total = [], [], 0
    for rows, turned, weights in groups:
        at = len(flat)
        flat.append(rows)
        for pair in weights:
            width = pair[0].shape[0 if turned else 1]
            plan.append((at, len(flat), turned, total, total + width))
            flat.extend(pair)
            total += width

    def body(*refs):
        own, up, down, low, high = refs[len(flat) :]
        for rows_at, pair_at, turned, start, stop in plan:
            cols = slice(start, stop)
            dims = (((1,), (1,)), ((), ())) if turned else (((1,), (0,)), ((), ()))
            for block in (2, 1, 3, 0):
                at = refs[rows_at][block * 256 : (block + 1) * 256]
                out = lax.dot_general(at[:, :512], refs[pair_at][...], dims, preferred_element_type=F32)
                out += lax.dot_general(at[:, 512:], refs[pair_at + 1][...], dims, preferred_element_type=F32)
                out = out.astype(BF)
                if block == 0:
                    own[:, cols] = out
                elif block == 1:
                    low[:, cols] = out[:128]
                    up[128:, cols] = out[128:]
                elif block == 2:
                    up[:128, cols] = out[:128]
                    down[:128, cols] = out[128:]
                else:
                    down[128:, cols] = out[:128]
                    high[:, cols] = out[128:]

    shapes = [((n, total), BF) for n in (256, 256, 256, 128, 128)]
    return kernel_call(body, shapes, *flat)


def add(left, right):
    return (left.astype(F32) + right.astype(F32)).astype(BF)


def ring_first(terms, axis="y"):
    return shift(terms[1], axis, 4, 1), shift(terms[2], axis, 4, -1)


def ring_second(terms, first, axis="y"):
    half = terms[3].shape[0]
    up, down = add(terms[3], first[0][:half]), add(terms[4], first[1][:half])
    return shift(up, axis, 4, 1), shift(down, axis, 4, -1)


def ring_sum(terms, first, second):
    own, half = terms[0].astype(F32), terms[3].shape[0]
    low = own[:half] + first[1][half:].astype(F32) + second[0].astype(F32)
    high = own[half:] + first[0][half:].astype(F32) + second[1].astype(F32)
    return jnp.concatenate([low, high])


def spread_first(own, axis="y"):
    return shift(own, axis, 4, 1), shift(own, axis, 4, -1)


def spread_second(first, axis="y"):
    half = first[0].shape[0] // 2
    return shift(first[0][:half], axis, 4, 1), shift(first[1][half:], axis, 4, -1)


def spread_all(own, first, second):
    return jnp.concatenate([own, first[1], second[0], second[1], first[0]])


def split_core(parts):
    def body(*refs):
        for half in range(2):
            cols = slice(half * 512, (half + 1) * 512)
            for y in range(4):
                for core in range(2):
                    at = slice(y * 256 + core * 128, y * 256 + core * 128 + 128)
                    total = refs[half][at]
                    for i in range(2 + half, len(parts), 2):
                        total += refs[i][at]
                    refs[len(parts) + core][y * 128 : (y + 1) * 128, cols] = total.astype(BF)

    return kernel_call(body, [((512, 1024), BF)] * 2, *parts)


def sum_core(keep, got):
    def body(*refs):
        own, up, down, low, high = refs[2:]
        for y in range(4):
            for x in range(4):
                at = slice((y * 4 + x) * 32, (y * 4 + x + 1) * 32)
                total = (refs[0][at].astype(F32) + refs[1][at].astype(F32)).astype(BF)
                half = slice(y % 2 * 32, y % 2 * 32 + 32)
                first = y < 2
                if x == 0:
                    own[y * 32 : (y + 1) * 32] = total
                elif x == 1:
                    (low if first else up.at[64:])[half] = total
                elif x == 2:
                    (up if first else down)[half] = total
                else:
                    (down.at[64:] if first else high)[half] = total

    return kernel_call(body, [((n, 1024), BF) for n in (128, 128, 128, 64, 64)], keep, got)


def sum_x(terms, first, second):
    def body(own, up, down, low, high, keep, send):
        for y in range(4):
            half = y % 2 * 32
            for z, out in enumerate((keep, send)):
                at = slice(half + z * 16, half + z * 16 + 16)
                far = slice(64 + half + z * 16, 64 + half + z * 16 + 16)
                total = own[y * 32 + z * 16 : y * 32 + z * 16 + 16].astype(F32)
                total += (down if y < 2 else up)[far].astype(F32)
                total += (low if y < 2 else high)[at].astype(F32)
                out[y * 16 : (y + 1) * 16] = total.astype(BF)

    return kernel_call(body, [((64, 1024), BF)] * 2, terms[0], *first, *second)


def add_to_rows(keep, got):
    def body(*refs):
        for y in range(4):
            at = slice(y * 16, (y + 1) * 16)
            refs[2 + y][...] = (refs[0][at].astype(F32) + refs[1][at].astype(F32)).astype(BF)

    return kernel_call(body, [((16, 1024), BF)] * 4, keep, got)


def final_add(own, other):
    def body(*refs):
        start = 0
        for ref in refs[1:-1]:
            at = slice(start, start + ref.shape[0])
            refs[-1][at] = refs[0][at] + ref[...].astype(F32)
            start += ref.shape[0]

    return kernel_call(body, [(own[0].shape, F32)], *own, *other)[0]


def together(first, *earlier):
    first = tuple(first)
    return lax.optimization_barrier(first + earlier)[: len(first)]


def input_terms(pgrad, weight, other_a, other_b):
    other = dot(pgrad[:, :SPLIT], other_a, ((1,), (1,))) + dot(pgrad[:, SPLIT:], other_b, ((1,), (1,)))
    return [dot(pgrad, weight, ((1,), (1,))), other]


def local(tokens, out_grad, gate_weight, up_weight, down_weight):
    gate = gate_weight[:, :SPLIT], gate_weight[:, SPLIT:]
    gate_a = swap(gate[0], "z_hi")
    groups = feature_groups([tokens, out_grad])
    mine = stack_rows([groups[0]] + [shift(groups[4 - j], "y", 4, -j) for j in (1, 2, 3)])
    mine = after(mine, gate_a)
    other = swap(mine, "z_lo")
    gate_b = swap(after(gate[1], other), "z_hi")
    down = down_weight[:256], down_weight[256:640], down_weight[640:]
    down_a = swap(after(down[0], other), "z_hi")
    mine = join_rows(mine, other)
    x_first = together(spread_first(mine, "x"), gate_b)
    down_b = swap(after(down[1], gate_b), "z_hi")
    x_second = together(spread_second(x_first, "x"), down_a, down_b)
    tok, cot = join_x(mine, x_first, x_second)
    down_c = swap(after(down[2], down_a), "z_hi")
    rows = join_core(tok, swap(tok, "core"))
    cotan = join_core(cot, swap(cot, "core"))
    up_other = swap(after(up_weight, down_b), "z_hi")

    gate_terms = forward([(rows, False, [(gate[0], gate_a), (gate[1], gate_b)])])
    gate_first = ring_first(gate_terms)
    cotan = after(cotan, gate_terms[0])
    grad_terms = forward([(cotan, True, list(zip(down, (down_a, down_b, down_c))))])
    grad_first = ring_first(grad_terms)
    gate_second = ring_second(gate_terms, gate_first)
    up_terms = forward([(after(rows, grad_terms[0], *gate_first), False, [(up_weight, up_other)])])
    grad_second = ring_second(grad_terms, grad_first)
    up_first = ring_first(up_terms)
    gate_pre = ring_sum(gate_terms, gate_first, gate_second)
    sigmoid_gate = jax.nn.sigmoid(gate_pre)
    activated = gate_pre * sigmoid_gate
    hidden_grad = ring_sum(grad_terms, grad_first, grad_second)

    up_pgrad = (hidden_grad * activated).astype(BF)
    spread_up = spread_first(up_pgrad)
    up_first = together(up_first, *spread_up)
    up_second = ring_second(up_terms, up_first)
    up_pre = ring_sum(up_terms, up_first, up_second)
    gate_pgrad = hidden_grad * up_pre * sigmoid_gate * (1.0 + gate_pre * (1.0 - sigmoid_gate))
    gate_pgrad = gate_pgrad.astype(BF)
    hidden = (activated * up_pre).astype(BF)
    far_up = spread_second(spread_up)
    spread_gate = spread_first(gate_pgrad)
    far_up = together(far_up, gate_pgrad)
    up_all = spread_all(up_pgrad, spread_up, far_up)
    up_far = dot(rows[:, 512:], up_all, ((0,), (0,))).astype(BF)
    up_got = [swap(up_far, "z_hi")]
    spread_gate = together(spread_gate, up_far)
    far_gate = spread_second(spread_gate)
    spread_hid = spread_first(after(hidden, *far_gate))
    input_up = [dot(up_all, up_weight, ((1,), (1,))), dot(up_all, up_other, ((1,), (1,)))]
    gate_all = spread_all(gate_pgrad, spread_gate, far_gate)
    gate_far = dot(rows[:, 512:], gate_all, ((0,), (0,))).astype(BF)
    gate_got = [swap(gate_far, "z_hi")]
    gate_all = after(gate_all, gate_far)

    input_gate = input_terms(gate_all, gate_weight, gate_a, gate_b)
    input_gate[0] = after(input_gate[0], *up_got)
    keep, send = split_core(input_up + input_gate)
    send = swap(send, "core")
    by_x = sum_core(keep, send)
    first = ring_first(by_x, "x")
    far_hid = spread_second(together(spread_hid, first[0]))
    second = ring_second(by_x, first, "x")
    second = together(second, gate_got[0], *far_hid)
    keep, send = sum_x(by_x, first, second)
    hid_all = spread_all(hidden, spread_hid, far_hid)
    near = jnp.concatenate([hidden, spread_hid[1], spread_hid[0]], axis=0)
    cot_near = jnp.concatenate([cotan[:512, 512:], cotan[768:, 512:]], axis=0)
    down_near = dot(near, cot_near, ((0,), (0,)))
    down_far = dot(jnp.concatenate(far_hid, axis=0), cotan[512:768, 512:], ((0,), (0,)))
    down_far = (down_near + down_far).astype(BF)
    got_z = swap(send, "z_lo")
    down_got = [swap(down_far, "z_hi")]
    by_y = add_to_rows(keep, got_z)
    input_grad = whole_rows([by_y[0]] + [shift(by_y[j], "y", 4, j) for j in (1, 2, 3)])
    rows_own = after(rows[:, :512], by_y[0])
    gate_own = dot(rows_own, gate_all, ((0,), (0,)))
    up_own = dot(rows_own, up_all, ((0,), (0,)))
    down_own = dot(hid_all, cotan[:, :512], ((0,), (0,)))
    return (
        input_grad,
        final_add([gate_own], gate_got),
        final_add([up_own], up_got),
        final_add([down_own], down_got),
    )


def solution(mesh):
    split = Mesh(mesh.devices.reshape(4, 2, 4, 2, 2), ("y", "z_hi", "x", "z_lo", "core"))
    fsdp, tsp = ("y", "z_hi"), ("x", "z_lo", "core")
    rows = P(fsdp + tsp, None)
    in_specs = (rows, rows, P(fsdp, tsp), P(fsdp, tsp), P(tsp, fsdp))
    out_specs = (rows, P(fsdp, tsp), P(fsdp, tsp), P(tsp, fsdp))
    return jax.shard_map(local, mesh=split, in_specs=in_specs, out_specs=out_specs, check_vma=False)
```

```python
import jax
import jax.numpy as jnp
from jax import lax
from jax.experimental import pallas as pl
from jax.experimental.pallas import tpu as pltpu
from jax.sharding import Mesh, PartitionSpec as P

BF = jnp.bfloat16
F32 = jnp.float32
SPLIT = 384
LIMIT = 20 * 1024 * 1024


def shift(value, axis, size, by):
    return lax.ppermute(value, axis, [(i, (i + by) % size) for i in range(size)])


def swap(value, axis):
    return shift(value, axis, 2, 1)


def after(value, *earlier):
    return lax.optimization_barrier((value,) + earlier)[0]


def dot(left, right, dims):
    return lax.dot_general(left, right, (dims, ((), ())), preferred_element_type=F32)


def kernel_call(body, shapes, *operands):
    spec = pl.BlockSpec(memory_space=pltpu.VMEM)
    return pl.pallas_call(
        body,
        out_shape=[jax.ShapeDtypeStruct(shape, kind) for shape, kind in shapes],
        in_specs=[spec] * len(operands),
        out_specs=[spec] * len(shapes),
        compiler_params=pltpu.CompilerParams(vmem_limit_bytes=LIMIT),
        cost_estimate=pl.CostEstimate(flops=0, bytes_accessed=0, transcendentals=0),
    )(*operands)


def feature_groups(pieces):
    count = len(pieces)

    def body(*refs):
        held, sems = refs[count + 4 : -1], refs[-1]
        copies = [pltpu.make_async_copy(refs[i], held[i], sems.at[i]) for i in range(count)]
        for copy in copies:
            copy.start()
        y, z_hi = lax.axis_index("y"), lax.axis_index("z_hi")
        for i in range(count):
            copies[i].wait()
            for k in range(4):
                for half in range(2):
                    at = pl.multiple_of(lax.rem(y + k, 4) * 1024 + lax.rem(z_hi + half, 2) * 512, 512)
                    refs[count + k][i * 16 : (i + 1) * 16, half * 512 : (half + 1) * 512] = held[i][:, pl.ds(at, 512)]

    return pl.pallas_call(
        body,
        out_shape=[jax.ShapeDtypeStruct((16 * count, 1024), BF)] * 4,
        in_specs=[pl.BlockSpec(memory_space=pl.ANY)] * count,
        out_specs=[pl.BlockSpec(memory_space=pltpu.VMEM)] * 4,
        scratch_shapes=[pltpu.VMEM((16, 4096), BF)] * count + [pltpu.SemaphoreType.DMA((count,))],
        compiler_params=pltpu.CompilerParams(vmem_limit_bytes=LIMIT),
        cost_estimate=pl.CostEstimate(flops=0, bytes_accessed=0, transcendentals=0),
    )(*pieces)


def whole_rows(groups):
    def body(*refs):
        y, z_hi = lax.axis_index("y"), lax.axis_index("z_hi")
        for k in range(4):
            for half in range(2):
                at = pl.multiple_of(lax.rem(y + 4 - k, 4) * 1024 + lax.rem(z_hi + half, 2) * 512, 512)
                refs[4][:, pl.ds(at, 512)] = refs[k][:, half * 512 : (half + 1) * 512]

    return kernel_call(body, [((16, 4096), BF)], *groups)[0]


def stack_rows(parts):
    def body(*refs):
        for y in range(4):
            refs[4][y * 32 : (y + 1) * 32] = refs[y][...]

    return kernel_call(body, [((128, 1024), BF)], *parts)[0]


def join_rows(mine, other):
    def body(mine_ref, other_ref, out_ref):
        out_ref[:128] = mine_ref[...]
        out_ref[128:] = other_ref[...]

    return kernel_call(body, [((256, 1024), BF)], mine, other)[0]


def join_x(own, first, second):
    def body(own_ref, minus, plus, low, high, *outs):
        for y in range(4):
            for x, ref in enumerate((own_ref, plus, None, minus)):
                for z in range(2):
                    for which in range(2):
                        to = (y * 4 + x) * 32 + z * 16
                        at = y * 32 + which * 16
                        if x == 2:
                            outs[which][to : to + 16] = (high if z else low)[at : at + 16]
                        else:
                            outs[which][to : to + 16] = ref[z * 128 + at : z * 128 + at + 16]

    return kernel_call(body, [((512, 1024), BF)] * 2, own, *first, *second)


def join_core(own, other):
    def body(own_ref, other_ref, out):
        for y in range(4):
            out[y * 256 : y * 256 + 128] = own_ref[y * 128 : (y + 1) * 128]
            out[y * 256 + 128 : (y + 1) * 256] = other_ref[y * 128 : (y + 1) * 128]

    return kernel_call(body, [((1024, 1024), BF)], own, other)[0]


def forward(groups):
    plan, flat, total = [], [], 0
    for rows, turned, weights in groups:
        at = len(flat)
        flat.append(rows)
        for pair in weights:
            width = pair[0].shape[0 if turned else 1]
            plan.append((at, len(flat), turned, total, total + width))
            flat.extend(pair)
            total += width

    def body(*refs):
        own, up, down, low, high = refs[len(flat) :]
        for rows_at, pair_at, turned, start, stop in plan:
            cols = slice(start, stop)
            dims = (((1,), (1,)), ((), ())) if turned else (((1,), (0,)), ((), ()))
            for block in (2, 1, 3, 0):
                at = refs[rows_at][block * 256 : (block + 1) * 256]
                out = lax.dot_general(at[:, :512], refs[pair_at][...], dims, preferred_element_type=F32)
                out += lax.dot_general(at[:, 512:], refs[pair_at + 1][...], dims, preferred_element_type=F32)
                out = out.astype(BF)
                if block == 0:
                    own[:, cols] = out
                elif block == 1:
                    low[:, cols] = out[:128]
                    up[128:, cols] = out[128:]
                elif block == 2:
                    up[:128, cols] = out[:128]
                    down[:128, cols] = out[128:]
                else:
                    down[128:, cols] = out[:128]
                    high[:, cols] = out[128:]

    shapes = [((n, total), BF) for n in (256, 256, 256, 128, 128)]
    return kernel_call(body, shapes, *flat)


def add(left, right):
    return (left.astype(F32) + right.astype(F32)).astype(BF)


def ring_first(terms, axis="y"):
    return shift(terms[1], axis, 4, 1), shift(terms[2], axis, 4, -1)


def ring_second(terms, first, axis="y"):
    half = terms[3].shape[0]
    up, down = add(terms[3], first[0][:half]), add(terms[4], first[1][:half])
    return shift(up, axis, 4, 1), shift(down, axis, 4, -1)


def ring_sum(terms, first, second):
    own, half = terms[0].astype(F32), terms[3].shape[0]
    low = own[:half] + first[1][half:].astype(F32) + second[0].astype(F32)
    high = own[half:] + first[0][half:].astype(F32) + second[1].astype(F32)
    return jnp.concatenate([low, high])


def spread_first(own, axis="y"):
    return shift(own, axis, 4, 1), shift(own, axis, 4, -1)


def spread_second(first, axis="y"):
    half = first[0].shape[0] // 2
    return shift(first[0][:half], axis, 4, 1), shift(first[1][half:], axis, 4, -1)


def spread_all(own, first, second):
    return jnp.concatenate([own, first[1], second[0], second[1], first[0]])


def split_core(parts):
    def body(*refs):
        for half in range(2):
            cols = slice(half * 512, (half + 1) * 512)
            for y in range(4):
                for core in range(2):
                    at = slice(y * 256 + core * 128, y * 256 + core * 128 + 128)
                    total = refs[half][at]
                    for i in range(2 + half, len(parts), 2):
                        total += refs[i][at]
                    refs[len(parts) + core][y * 128 : (y + 1) * 128, cols] = total.astype(BF)

    return kernel_call(body, [((512, 1024), BF)] * 2, *parts)


def sum_core(keep, got):
    def body(*refs):
        own, up, down, low, high = refs[2:]
        for y in range(4):
            for x in range(4):
                at = slice((y * 4 + x) * 32, (y * 4 + x + 1) * 32)
                total = (refs[0][at].astype(F32) + refs[1][at].astype(F32)).astype(BF)
                half = slice(y % 2 * 32, y % 2 * 32 + 32)
                first = y < 2
                if x == 0:
                    own[y * 32 : (y + 1) * 32] = total
                elif x == 1:
                    (low if first else up.at[64:])[half] = total
                elif x == 2:
                    (up if first else down)[half] = total
                else:
                    (down.at[64:] if first else high)[half] = total

    return kernel_call(body, [((n, 1024), BF) for n in (128, 128, 128, 64, 64)], keep, got)


def sum_x(terms, first, second):
    def body(own, up, down, low, high, keep, send):
        for y in range(4):
            half = y % 2 * 32
            for z, out in enumerate((keep, send)):
                at = slice(half + z * 16, half + z * 16 + 16)
                far = slice(64 + half + z * 16, 64 + half + z * 16 + 16)
                total = own[y * 32 + z * 16 : y * 32 + z * 16 + 16].astype(F32)
                total += (down if y < 2 else up)[far].astype(F32)
                total += (low if y < 2 else high)[at].astype(F32)
                out[y * 16 : (y + 1) * 16] = total.astype(BF)

    return kernel_call(body, [((64, 1024), BF)] * 2, terms[0], *first, *second)


def add_to_rows(keep, got):
    def body(*refs):
        for y in range(4):
            at = slice(y * 16, (y + 1) * 16)
            refs[2 + y][...] = (refs[0][at].astype(F32) + refs[1][at].astype(F32)).astype(BF)

    return kernel_call(body, [((16, 1024), BF)] * 4, keep, got)


def final_add(own, other):
    def body(*refs):
        start = 0
        for ref in refs[1:-1]:
            at = slice(start, start + ref.shape[0])
            refs[-1][at] = refs[0][at] + ref[...].astype(F32)
            start += ref.shape[0]

    return kernel_call(body, [(own[0].shape, F32)], *own, *other)[0]


def together(first, *earlier):
    first = tuple(first)
    return lax.optimization_barrier(first + earlier)[: len(first)]


def input_terms(pgrad, weight, other_a, other_b):
    other = dot(pgrad[:, :SPLIT], other_a, ((1,), (1,))) + dot(pgrad[:, SPLIT:], other_b, ((1,), (1,)))
    return [dot(pgrad, weight, ((1,), (1,))), other]


def local(tokens, out_grad, gate_weight, up_weight, down_weight):
    gate = gate_weight[:, :SPLIT], gate_weight[:, SPLIT:]
    gate_a = swap(gate[0], "z_hi")
    groups = feature_groups([tokens, out_grad])
    mine = stack_rows([groups[0]] + [shift(groups[4 - j], "y", 4, -j) for j in (1, 2, 3)])
    mine = after(mine, gate_a)
    other = swap(mine, "z_lo")
    gate_b = swap(after(gate[1], other), "z_hi")
    down = down_weight[:256], down_weight[256:640], down_weight[640:]
    down_a = swap(after(down[0], other), "z_hi")
    mine = join_rows(mine, other)
    x_first = together(spread_first(mine, "x"), gate_b)
    down_b = swap(after(down[1], gate_b), "z_hi")
    x_second = together(spread_second(x_first, "x"), down_a, down_b)
    tok, cot = join_x(mine, x_first, x_second)
    down_c = swap(after(down[2], down_a), "z_hi")
    rows = join_core(tok, swap(tok, "core"))
    cotan = join_core(cot, swap(cot, "core"))
    up_other = swap(after(up_weight, down_b), "z_hi")

    gate_terms = forward([(rows, False, [(gate[0], gate_a), (gate[1], gate_b)])])
    gate_first = ring_first(gate_terms)
    cotan = after(cotan, gate_terms[0])
    grad_terms = forward([(cotan, True, list(zip(down, (down_a, down_b, down_c))))])
    grad_first = ring_first(grad_terms)
    gate_second = ring_second(gate_terms, gate_first)
    up_terms = forward([(after(rows, grad_terms[0], *gate_first), False, [(up_weight, up_other)])])
    grad_second = ring_second(grad_terms, grad_first)
    up_first = ring_first(up_terms)
    gate_pre = ring_sum(gate_terms, gate_first, gate_second)
    sigmoid_gate = jax.nn.sigmoid(gate_pre)
    activated = gate_pre * sigmoid_gate
    hidden_grad = ring_sum(grad_terms, grad_first, grad_second)

    up_pgrad = (hidden_grad * activated).astype(BF)
    spread_up = spread_first(up_pgrad)
    up_first = together(up_first, *spread_up)
    up_second = ring_second(up_terms, up_first)
    up_pre = ring_sum(up_terms, up_first, up_second)
    gate_pgrad = hidden_grad * up_pre * sigmoid_gate * (1.0 + gate_pre * (1.0 - sigmoid_gate))
    gate_pgrad = gate_pgrad.astype(BF)
    hidden = (activated * up_pre).astype(BF)
    far_up = spread_second(spread_up)
    spread_gate = spread_first(gate_pgrad)
    far_up = together(far_up, gate_pgrad)
    up_all = spread_all(up_pgrad, spread_up, far_up)
    up_part = jnp.concatenate([up_pgrad, spread_up[1], spread_up[0]], axis=0)
    rows_part = jnp.concatenate([rows[:512, 512:], rows[768:, 512:]], axis=0)
    up_near = dot(rows_part, up_part, ((0,), (0,)))
    up_far = dot(rows[512:768, 512:], jnp.concatenate(far_up, axis=0), ((0,), (0,)))
    up_far = (up_near + up_far).astype(BF)
    up_got = [swap(up_far, "z_hi")]
    spread_gate = together(spread_gate, up_far)
    far_gate = spread_second(spread_gate)
    spread_hid = spread_first(after(hidden, *far_gate))
    input_up = [dot(up_all, up_weight, ((1,), (1,))), dot(up_all, up_other, ((1,), (1,)))]
    gate_all = spread_all(gate_pgrad, spread_gate, far_gate)
    near = jnp.concatenate([gate_pgrad, spread_gate[1], spread_gate[0]], axis=0)
    rows_near = jnp.concatenate([rows[:512, 512:], rows[768:, 512:]], axis=0)
    gate_near = dot(rows_near, near, ((0,), (0,)))
    gate_far = dot(rows[512:768, 512:], jnp.concatenate(far_gate, axis=0), ((0,), (0,)))
    gate_far = (gate_near + gate_far).astype(BF)
    gate_got = [swap(gate_far, "z_hi")]
    gate_all = after(gate_all, gate_far)

    input_gate = input_terms(gate_all, gate_weight, gate_a, gate_b)
    input_gate[0] = after(input_gate[0], *up_got)
    keep, send = split_core(input_up + input_gate)
    send = swap(send, "core")
    by_x = sum_core(keep, send)
    first = ring_first(by_x, "x")
    far_hid = spread_second(together(spread_hid, first[0]))
    second = ring_second(by_x, first, "x")
    second = together(second, gate_got[0], *far_hid)
    keep, send = sum_x(by_x, first, second)
    hid_all = spread_all(hidden, spread_hid, far_hid)
    near = jnp.concatenate([hidden, spread_hid[1], spread_hid[0]], axis=0)
    cot_near = jnp.concatenate([cotan[:512, 512:], cotan[768:, 512:]], axis=0)
    down_near = dot(near, cot_near, ((0,), (0,)))
    down_far = dot(jnp.concatenate(far_hid, axis=0), cotan[512:768, 512:], ((0,), (0,)))
    down_far = (down_near + down_far).astype(BF)
    got_z = swap(send, "z_lo")
    down_got = [swap(down_far, "z_hi")]
    by_y = add_to_rows(keep, got_z)
    input_grad = whole_rows([by_y[0]] + [shift(by_y[j], "y", 4, j) for j in (1, 2, 3)])
    rows_own = after(rows[:, :512], by_y[0])
    gate_own = dot(rows_own, gate_all, ((0,), (0,)))
    up_own = dot(rows_own, up_all, ((0,), (0,)))
    down_own = dot(hid_all, cotan[:, :512], ((0,), (0,)))
    return (
        input_grad,
        final_add([gate_own], gate_got),
        final_add([up_own], up_got),
        final_add([down_own], down_got),
    )


def solution(mesh):
    split = Mesh(mesh.devices.reshape(4, 2, 4, 2, 2), ("y", "z_hi", "x", "z_lo", "core"))
    fsdp, tsp = ("y", "z_hi"), ("x", "z_lo", "core")
    rows = P(fsdp + tsp, None)
    in_specs = (rows, rows, P(fsdp, tsp), P(fsdp, tsp), P(tsp, fsdp))
    out_specs = (rows, P(fsdp, tsp), P(fsdp, tsp), P(tsp, fsdp))
    return jax.shard_map(local, mesh=split, in_specs=in_specs, out_specs=out_specs, check_vma=False)
```
